512 devices in a mesh: orig: 128 (over y, z, core), link: 4 (over x).
Axes of the slice: x: 4, y: 4, z: 16, core: 2. Of those that a mesh axis runs over, the one named last changes fastest.
Arguments:
- background: bfloat16 [262144, 256], P('orig'), may hold values from -6 to 6
- live_counts: int32 [2048], P('orig'), may hold values from 1 to 128
- patterns: bfloat16 [4, 4096, 128, 128], P('link', 'orig'), may hold values from -0.009765625 to 0.009765625
- pattern_ids: int32 [4, 2048, 12], P('link', 'orig'), may hold values from 0 to 31
- link_targets: int32 [4, 2048, 12], P('link', 'orig'), may hold values from 0 to 7
- counts_obs: float32 [4, 1024], P('link', 'orig'), may hold values from -6 to 6
- obs_var: float32 [4, 1024], P('link', 'orig'), may hold values from 1 to 10
Outputs:
- analysis: bfloat16 [262144, 256], P(('orig', 'link'))
The draws below stay inside these ranges and needn't reach their ends.
All inputs are finite; a program needn't handle non-finite values. Where the reference program divides by a largest or mean magnitude, that divisor is 1e-20 or more.
Results may differ from the reference program's by a relative error of at most 0.001.
Values sent between devices are 32-bit elements; how exact they have to be, the bound alone decides.
No kernel may reach another device: no remote copies, remote signals or barrier semaphores. Data moves between devices by JAX's collectives and lax.ppermute only.
A program may use at most 64 MiB of HBM per device.

```python
import math
import jax
import jax.numpy as jnp
from jax import lax

M = 256
SB = 128
NB_DEV = 16
TPB = 12
NPAT_DEV = 32
LB = 128
NLB = 8
NS_ITERS = 4
BLOCKS = 2048
STATES = 262144
PATTERNS = 4096
LINKS = 1024
N_ORIG = 128
N_LINK = 4


def touch_ends(array, own_key, least, high):
    dims = array.shape
    index_at = [jax.random.randint(jax.random.fold_in(own_key, axis), (), 0, dims[axis]) for axis in range(len(dims))]
    array = array.at[tuple(index_at)].set(least)
    longest = dims.index(max(dims))
    index_at[longest] = (index_at[longest] + 1) % dims[longest]
    return array.at[tuple(index_at)].set(high)


def levels(stream_key, dims, shards, smallest, largest):
    loudness = 1.0
    for dim, shards_of in shards:
        draws = jax.random.uniform(jax.random.fold_in(jax.random.fold_in(stream_key, 6), dim), (shards_of,), jnp.float32, smallest / len(shards), largest / len(shards))
        loudness = loudness * jnp.repeat(jnp.exp(draws), dims[dim] // shards_of).reshape((-1,) + (1,) * (len(dims) - 1 - dim))
    return loudness


def noise(stream_key, shape, scale, bound, split=(), held_as=jnp.bfloat16):
    gain = levels(stream_key, shape, split, -0.22, 0.18) if split else 1.0
    result = jax.random.normal(stream_key, shape, jnp.float32) * scale * gain
    return jnp.minimum(jnp.maximum(result, -bound), bound).astype(held_as)


def setup_inputs(seed: int = 0) -> dict:
    splits = jax.random.split(jax.random.key(seed), 8)
    background = noise(splits[0], (STATES, M), 1.0, 6.0, ((0, 128),))
    live_counts = touch_ends(jax.random.randint(splits[1], (BLOCKS,), 1, SB + 1), jax.random.fold_in(splits[1], 1), 1, SB).astype(jnp.int32)
    patterns = noise(splits[2], (N_LINK, PATTERNS, LB, SB), (SB * TPB * NB_DEV * N_ORIG // NLB) ** -0.5, 0.009765625, ((0, 4), (1, 128)))
    pattern_ids = touch_ends(jax.random.randint(splits[3], (N_LINK, BLOCKS, TPB), 0, NPAT_DEV), jax.random.fold_in(splits[3], 1), 0, NPAT_DEV - 1).astype(jnp.int32)
    link_targets = touch_ends(jax.random.randint(splits[4], (N_LINK, BLOCKS, TPB), 0, NLB), jax.random.fold_in(splits[4], 1), 0, NLB - 1).astype(jnp.int32)
    counts_obs = noise(splits[5], (N_LINK, LINKS), 1.0, 6.0, ((0, 4), (1, 128)), jnp.float32)
    obs_var = jnp.clip(jnp.exp(math.log(10.0) - 2.3025851 * jax.random.uniform(splits[6], (N_LINK, LINKS), jnp.float32) ** levels(splits[6], (N_LINK, LINKS), ((0, 4), (1, 128)), -0.2, 0.2)), 1.0, 10.0)
    return dict(background=background, live_counts=live_counts, patterns=patterns, pattern_ids=pattern_ids, link_targets=link_targets, counts_obs=counts_obs, obs_var=obs_var)


def transform_of(ensemble_gram, forcing):
    members = ensemble_gram.shape[0]
    identity = jnp.eye(members, dtype=jnp.float32)
    system = identity + ensemble_gram / (members - 1.0)
    row_bound = jnp.max(lax.optimization_barrier(jnp.sum(jnp.abs(system), axis=1)))
    square_root = system / row_bound
    inverse = identity
    for sweep_index in range(NS_ITERS):
        middle = 0.5 * (3.0 * identity - jnp.dot(inverse, square_root, precision=lax.Precision.HIGHEST))
        square_root = jnp.dot(square_root, middle, precision=lax.Precision.HIGHEST)
        inverse = jnp.dot(middle, inverse, precision=lax.Precision.HIGHEST)
    spread_weights = inverse / jnp.sqrt(row_bound)
    inner = jnp.dot(inverse, forcing, precision=lax.Precision.HIGHEST)
    mean_weights = jnp.dot(inverse, inner, precision=lax.Precision.HIGHEST) / (row_bound * (members - 1.0))
    return spread_weights + mean_weights[:, None]

def group_predictions(group_index, masked, patterns, pattern_ids, link_targets):
    tile_bank = patterns[group_index]
    shard_states = masked.reshape(N_ORIG, NB_DEV, SB, M)
    shard_ids = pattern_ids[group_index].reshape(N_ORIG, NB_DEV, TPB)
    shard_targets = link_targets[group_index].reshape(N_ORIG, NB_DEV, TPB)
    block_numbers = jnp.arange(NLB, dtype=jnp.int32)

    def add_shard(running, inputs):
        shard_index, states_part, tile_ids, targets = inputs
        global_ids = (tile_ids + shard_index * NPAT_DEV).astype(jnp.int32)
        chosen = jnp.take(tile_bank, global_ids, axis=0).astype(jnp.float32)
        products = jnp.einsum('btls,bsm->btlm', chosen, states_part.astype(jnp.float32), precision=lax.Precision.HIGHEST)
        onehot = (targets[:, :, None] == block_numbers[None, None, :]).astype(jnp.float32)
        return (running + jnp.einsum('btj,btlm->jlm', onehot, products, precision=lax.Precision.HIGHEST), None)
    start = jnp.zeros((NLB, LB, M), jnp.float32)
    shard_numbers = jnp.arange(N_ORIG, dtype=jnp.int32)
    total, unused = lax.scan(add_shard, start, (shard_numbers, shard_states, shard_ids, shard_targets))
    return total.reshape(NLB * LB, M)

def reference(background, live_counts, patterns, pattern_ids, link_targets, counts_obs, obs_var):
    position = jnp.arange(SB, dtype=jnp.int32)
    living = position[None, :] < live_counts[:, None]
    masked = background.reshape(BLOCKS, SB, M) * living[:, :, None].astype(jnp.bfloat16)

    def one_group(group_index):
        return group_predictions(group_index, masked, patterns, pattern_ids, link_targets)
    predicted = lax.map(one_group, jnp.arange(N_LINK, dtype=jnp.int32))
    pred_mean = lax.optimization_barrier(jnp.mean(predicted, axis=2))
    spread = (predicted - pred_mean[:, :, None]).reshape(N_LINK * LINKS, M)
    weights = (1.0 / obs_var).reshape(N_LINK * LINKS)
    innovation = (counts_obs - pred_mean).reshape(N_LINK * LINKS)
    ensemble_gram = jnp.dot(spread.T, spread * weights[:, None], precision=lax.Precision.HIGHEST)
    forcing = jnp.dot(spread.T, weights * innovation, precision=lax.Precision.HIGHEST)
    transform_mat = transform_of(ensemble_gram, forcing)
    states_f = background.astype(jnp.float32)
    centre = lax.optimization_barrier(jnp.mean(states_f, axis=1, keepdims=True))
    updated = centre + jnp.dot(states_f - centre, transform_mat, precision=lax.Precision.HIGHEST)
    live_flat = living.reshape(STATES)
    return jnp.where(live_flat[:, None], updated, states_f).astype(jnp.bfloat16)
```

```python
import functools

import jax
import jax.numpy as jnp
from jax import lax
from jax.experimental import pallas as pl
from jax.experimental.pallas import tpu as pltpu
from jax.sharding import Mesh
from jax.sharding import PartitionSpec as P

NLB = 8
NS_ITERS = 4
F32 = jnp.float32
BF16 = jnp.bfloat16
ORIG = ("y", "zh", "zl", "c")
SLAB = ("x", "y", "zl", "c")
VMEM = pl.BlockSpec(memory_space=pltpu.VMEM)
SMEM = pl.BlockSpec(memory_space=pltpu.SMEM)
PARAMS = pltpu.CompilerParams(vmem_limit_bytes=40 * 2**20)


def halves(a):
    high = a.astype(BF16)
    return high, (a - high.astype(F32)).astype(BF16)


def dot(a, b):
    return jnp.dot(a, b, preferred_element_type=F32)


def dot3(a, b):
    (ah, al), (bh, bl) = a, b
    return dot(ah, bh) + (dot(ah, bl) + dot(al, bh))


def term_kernel(me_ref, ids_ref, targets_ref, live_ref, states_ref, tiles_ref, keep_ref, send_ref):
    blocks, slots = ids_ref.shape
    block_rows = tiles_ref.shape[2]
    keep_ref[...] = jnp.zeros_like(keep_ref)
    send_ref[...] = jnp.zeros_like(send_ref)

    def run(by_core):
        def add_block(b, carry):
            rows = pl.ds(pl.multiple_of(b * block_rows, block_rows), block_rows)
            position = lax.broadcasted_iota(jnp.int32, (block_rows, states_ref.shape[1]), 0)
            living = (position < live_ref[b]).astype(F32).astype(BF16)
            masked = states_ref[rows, :] * living
            for t in range(slots):
                product = dot(tiles_ref[ids_ref[b, t]], masked)
                target = targets_ref[b, t]
                chunk = (target // 2) * 2
                first = (target % 2) * 32
                for g in range(16):
                    q, zl, c = g // 4, (g // 2) % 2, g % 2
                    at = pl.ds(pl.multiple_of(first + q * 8, 8), 8)
                    by_core[c][chunk + zl, at, :] += product[g * 8 : g * 8 + 8]
            return carry

        lax.fori_loop(0, blocks, add_block, 0)

    @pl.when(me_ref[0] == 0)
    def _():
        run((keep_ref, send_ref))

    @pl.when(me_ref[0] == 1)
    def _():
        run((send_ref, keep_ref))


def rows_kernel(parts_ref, counts_ref, var_ref, out_ref):
    total = jnp.sum(parts_ref[...], axis=0)
    rows = total.shape[0]
    out_ref[0:rows, :] = total[:, :128]
    out_ref[rows : 2 * rows, :] = total[:, 128:]
    lane = lax.broadcasted_iota(jnp.int32, (8, 128), 1)
    tail = jnp.where(lane == 0, counts_ref[...], jnp.where(lane == 1, var_ref[...], 0.0))
    out_ref[2 * rows : 2 * rows + 8, :] = tail


def gram_kernel(parts_ref, out_ref):
    rows = (parts_ref.shape[1] - 8) // 2
    left = jnp.sum(parts_ref[:, 0:rows, :], axis=0)
    right = jnp.sum(parts_ref[:, rows : 2 * rows, :], axis=0)
    tail = parts_ref[:, 2 * rows :, :].reshape(rows, 128)
    counts, variance = tail[:, 0:1], tail[:, 1:2]
    mean = jnp.sum(left + right, axis=1, keepdims=True) * (1.0 / 256.0)
    spread = jnp.concatenate([left - mean, right - mean], axis=1)
    weights = 1.0 / variance
    forcing = jnp.sum(spread * (weights * (counts - mean)), axis=0, keepdims=True)
    gram = dot3(halves(spread.T), halves(spread * weights))
    out_ref[...] = jnp.zeros_like(out_ref)
    out_ref[0:16] = gram[:128, :128].reshape(16, 8, 128)
    out_ref[16:32] = gram[:128, 128:].reshape(16, 8, 128)
    out_ref[32:48] = gram[128:, 128:].reshape(16, 8, 128)
    out_ref[48, 0:1, :] = forcing[:, :128]
    out_ref[48, 1:2, :] = forcing[:, 128:]


def share_kernel(parts_ref, out_ref):
    total = jnp.sum(parts_ref[...], axis=0)
    out_ref[...] = jnp.broadcast_to(total[None], out_ref.shape)


def update_kernel(link_ref, live_ref, pieces_ref, states_ref, out_ref):
    members = states_ref.shape[1]
    first = pieces_ref[0:16].reshape(128, 128)
    across = pieces_ref[16:32].reshape(128, 128)
    last = pieces_ref[32:48].reshape(128, 128)
    gram = jnp.concatenate(
        [jnp.concatenate([first, across], axis=1), jnp.concatenate([across.T, last], axis=1)], axis=0
    )
    forcing = jnp.concatenate([pieces_ref[48, 0:1, :], pieces_ref[48, 1:2, :]], axis=1)
    at = lambda dim: lax.broadcasted_iota(jnp.int32, (members, members), dim)
    identity = jnp.where(at(0) == at(1), 1.0, 0.0).astype(F32)
    system = identity + gram * (1.0 / (members - 1.0))
    bound = jnp.max(jnp.sum(jnp.abs(system), axis=0, keepdims=True), axis=1, keepdims=True)
    root = system * (1.0 / bound)
    inverse = identity
    for sweep in range(NS_ITERS):
        if sweep == 0:
            middle = 1.5 * identity - 0.5 * root
            inverse = middle
        else:
            middle = 1.5 * identity - 0.5 * dot3(halves(inverse), halves(root))
        middle_halves = halves(middle)
        if sweep > 0:
            inverse = dot3(middle_halves, halves(inverse))
        if sweep < NS_ITERS - 1:
            root = dot3(halves(root), middle_halves)
    inner = dot3(halves(jnp.broadcast_to(forcing, (8, members))), halves(inverse))[0:1]
    mean_weights = jnp.sum(inverse * inner, axis=1, keepdims=True) * (1.0 / (bound * (members - 1.0)))
    transform = inverse * lax.rsqrt(bound) + mean_weights
    transform += (1.0 - jnp.sum(transform, axis=0, keepdims=True)) * (1.0 / members)
    high, low = halves(transform)
    states = states_ref[...]
    updated = dot(states, high) + dot(states, low)
    own_blocks = states.shape[0] // 128
    position = lax.broadcasted_iota(jnp.int32, (128, members), 0)
    for k in range(own_blocks):
        rows = slice(k * 128, k * 128 + 128)
        live = live_ref[link_ref[0] * own_blocks + k]
        kept = states[rows].astype(F32)
        out_ref[rows, :] = jnp.where(position < live, updated[rows], kept).astype(BF16)


def all_to_all(x, axes):
    return lax.all_to_all(x, axes, split_axis=0, concat_axis=0, tiled=True)


def per_device(background, live_counts, patterns, pattern_ids, link_targets, counts_obs, obs_var):
    states_dev, members = background.shape
    core = lax.axis_index("c").astype(jnp.int32).reshape(1)
    link = lax.axis_index("x").astype(jnp.int32).reshape(1)
    half = jax.ShapeDtypeStruct((8, 64, members), F32)
    keep, send = pl.pallas_call(
        term_kernel,
        out_shape=(half, half),
        in_specs=[SMEM, SMEM, SMEM, SMEM, VMEM, VMEM],
        out_specs=(VMEM, VMEM),
        compiler_params=PARAMS,
        name="term",
    )(core, pattern_ids[0], link_targets[0], live_counts, background, patterns[0])
    of_chip = keep + lax.ppermute(send, "c", [(0, 1), (1, 0)])
    parts = all_to_all(of_chip, ("y", "zl"))
    own = pl.pallas_call(
        rows_kernel,
        out_shape=jax.ShapeDtypeStruct((136, 128), F32),
        in_specs=[VMEM, VMEM, VMEM],
        out_specs=VMEM,
        compiler_params=PARAMS,
        name="rows",
    )(parts, counts_obs.reshape(8, 1), obs_var.reshape(8, 1))
    column = lax.all_gather(own, "zh")
    gram = pl.pallas_call(
        gram_kernel,
        out_shape=jax.ShapeDtypeStruct((64, 8, 128), F32),
        in_specs=[VMEM],
        out_specs=VMEM,
        compiler_params=PARAMS,
        name="gram",
    )(column)
    shared = pl.pallas_call(
        share_kernel,
        out_shape=jax.ShapeDtypeStruct((64, 8, 128), F32),
        in_specs=[VMEM],
        out_specs=VMEM,
        compiler_params=PARAMS,
        name="share",
    )(all_to_all(gram, SLAB))
    pieces = all_to_all(shared, SLAB)
    own_rows = states_dev // lax.axis_size("x")
    return pl.pallas_call(
        update_kernel,
        out_shape=jax.ShapeDtypeStruct((own_rows, members), BF16),
        grid_spec=pltpu.PrefetchScalarGridSpec(
            num_scalar_prefetch=2,
            grid=(1,),
            in_specs=[
                pl.BlockSpec((64, 8, 128), lambda i, link, live: (0, 0, 0)),
                pl.BlockSpec((own_rows, members), lambda i, link, live: (link[0], 0)),
            ],
            out_specs=pl.BlockSpec((own_rows, members), lambda i, link, live: (0, 0)),
        ),
        compiler_params=PARAMS,
        name="update",
    )(link, live_counts, pieces, background)


def solution(mesh):
    torus = Mesh(mesh.devices.reshape(4, 8, 2, 2, 4), ("y", "zh", "zl", "c", "x"))
    return jax.shard_map(
        per_device,
        mesh=torus,
        in_specs=(
            P(ORIG, None),
            P(ORIG),
            P("x", ORIG, None, None),
            P("x", ORIG, None),
            P("x", ORIG, None),
            P("x", ORIG),
            P("x", ORIG),
        ),
        out_specs=P((*ORIG, "x"), None),
        check_vma=False,
    )
```

```python
import jax
import jax.numpy as jnp
from jax import lax
from jax.experimental import pallas as pl
from jax.experimental.pallas import tpu as pltpu
from jax.sharding import Mesh
from jax.sharding import PartitionSpec as P

NLB = 8
NS_ITERS = 4
F32 = jnp.float32
BF16 = jnp.bfloat16
ORIG = ("y", "zh", "zl", "c")
SLAB = ("x", "y", "zl", "c")
VMEM = pl.BlockSpec(memory_space=pltpu.VMEM)
SMEM = pl.BlockSpec(memory_space=pltpu.SMEM)
PARAMS = pltpu.CompilerParams(vmem_limit_bytes=40 * 2**20)


def halves(a):
    high = a.astype(BF16)
    return high, (a - high.astype(F32)).astype(BF16)


def dot(a, b):
    return jnp.dot(a, b, preferred_element_type=F32)


def dot3(a, b):
    (ah, al), (bh, bl) = a, b
    return dot(ah, bh) + (dot(ah, bl) + dot(al, bh))


def term_kernel(me_ref, ids_ref, targets_ref, live_ref, states_ref, tiles_ref, keep_ref, send_ref):
    blocks, slots = ids_ref.shape
    block_rows = tiles_ref.shape[2]
    keep_ref[...] = jnp.zeros_like(keep_ref)
    send_ref[...] = jnp.zeros_like(send_ref)

    def run(by_core):
        def add_block(b, carry):
            rows = pl.ds(pl.multiple_of(b * block_rows, block_rows), block_rows)
            position = lax.broadcasted_iota(jnp.int32, (block_rows, states_ref.shape[1]), 0)
            living = (position < live_ref[b]).astype(F32).astype(BF16)
            masked = states_ref[rows, :] * living
            for t in range(slots):
                product = dot(tiles_ref[ids_ref[b, t]], masked)
                target = targets_ref[b, t]
                chunk = (target // 2) * 2
                first = (target % 2) * 32
                for g in range(16):
                    q, zl, c = g // 4, (g // 2) % 2, g % 2
                    at = pl.ds(pl.multiple_of(first + q * 8, 8), 8)
                    by_core[c][chunk + zl, at, :] += product[g * 8 : g * 8 + 8]
            return carry

        lax.fori_loop(0, blocks, add_block, 0)

    @pl.when(me_ref[0] == 0)
    def _():
        run((keep_ref, send_ref))

    @pl.when(me_ref[0] == 1)
    def _():
        run((send_ref, keep_ref))


def rows_kernel(parts_ref, out_ref):
    total = jnp.sum(parts_ref[...], axis=0)
    out_ref[...] = total.reshape(out_ref.shape)


def as_column(ref):
    count = ref.shape[1]
    at = lambda dim: lax.broadcasted_iota(jnp.int32, (count, count), dim)
    return jnp.sum(jnp.where(at(0) == at(1), ref[...], 0.0), axis=1, keepdims=True)


def gram_kernel(parts_ref, counts_ref, var_ref, out_ref):
    total = jnp.sum(parts_ref[...], axis=0)
    mean = jnp.mean(total, axis=1, keepdims=True)
    spread = total - mean
    weights = 1.0 / as_column(var_ref)
    forcing = jnp.sum(spread * (weights * (as_column(counts_ref) - mean)), axis=0, keepdims=True)
    gram = dot3(halves(spread.T), halves(spread * weights))
    out_ref[49:] = jnp.zeros((15, 8, 128), F32)
    out_ref[0:16] = gram[:128, :128].reshape(16, 8, 128)
    out_ref[16:32] = gram[:128, 128:].reshape(16, 8, 128)
    out_ref[32:48] = gram[128:, 128:].reshape(16, 8, 128)
    out_ref[48] = jnp.concatenate([forcing[:, :128], forcing[:, 128:], jnp.zeros((6, 128), F32)], axis=0)


def share_kernel(parts_ref, out_ref):
    total = jnp.sum(parts_ref[...], axis=0)
    out_ref[...] = jnp.broadcast_to(total[None], out_ref.shape)


def update_kernel(link_ref, live_ref, pieces_ref, states_ref, out_ref):
    members = states_ref.shape[1]
    first = pieces_ref[0:16].reshape(128, 128)
    across = pieces_ref[16:32].reshape(128, 128)
    last = pieces_ref[32:48].reshape(128, 128)
    gram = jnp.concatenate(
        [jnp.concatenate([first, across], axis=1), jnp.concatenate([across.T, last], axis=1)], axis=0
    )
    forcing = jnp.concatenate([pieces_ref[48, 0:1, :], pieces_ref[48, 1:2, :]], axis=1)
    at = lambda dim: lax.broadcasted_iota(jnp.int32, (members, members), dim)
    identity = jnp.where(at(0) == at(1), 1.0, 0.0).astype(F32)
    system = identity + gram * (1.0 / (members - 1.0))
    bound = jnp.max(jnp.sum(jnp.abs(system), axis=0, keepdims=True), axis=1, keepdims=True)
    root = system * (1.0 / bound)
    inverse = identity
    for sweep in range(NS_ITERS):
        if sweep == 0:
            middle = 1.5 * identity - 0.5 * root
            inverse = middle
        else:
            middle = 1.5 * identity - 0.5 * dot3(halves(inverse), halves(root))
        middle_halves = halves(middle)
        if sweep > 0:
            inverse = dot3(middle_halves, halves(inverse))
        if sweep < NS_ITERS - 1:
            root = dot3(halves(root), middle_halves)
    inner = dot3(halves(jnp.broadcast_to(forcing, (8, members))), halves(inverse))[0:1]
    mean_weights = jnp.sum(inverse * inner, axis=1, keepdims=True) * (1.0 / (bound * (members - 1.0)))
    transform = inverse * lax.rsqrt(bound) + mean_weights
    transform += (1.0 - jnp.sum(transform, axis=0, keepdims=True)) * (1.0 / members)
    high, low = halves(transform)
    states = states_ref[...]
    updated = dot(states, high) + dot(states, low)
    own_blocks = states.shape[0] // 128
    position = lax.broadcasted_iota(jnp.int32, (128, members), 0)
    for k in range(own_blocks):
        rows = slice(k * 128, k * 128 + 128)
        live = live_ref[link_ref[0] * own_blocks + k]
        kept = states[rows].astype(F32)
        out_ref[rows, :] = jnp.where(position < live, updated[rows], kept).astype(BF16)


def all_to_all(x, axes):
    return lax.all_to_all(x, axes, split_axis=0, concat_axis=0, tiled=True)


def local(kernel, shape, operands):
    return pl.pallas_call(
        kernel,
        out_shape=jax.ShapeDtypeStruct(shape, F32),
        in_specs=[VMEM] * operands,
        out_specs=VMEM,
        compiler_params=PARAMS,
        name=kernel.__name__,
    )


def per_device(background, live_counts, patterns, pattern_ids, link_targets, counts_obs, obs_var):
    states_dev, members = background.shape
    core = lax.axis_index("c").astype(jnp.int32).reshape(1)
    link = lax.axis_index("x").astype(jnp.int32).reshape(1)
    half = jax.ShapeDtypeStruct((8, 64, members), F32)
    keep, send = pl.pallas_call(
        term_kernel,
        out_shape=(half, half),
        in_specs=[SMEM, SMEM, SMEM, SMEM, VMEM, VMEM],
        out_specs=(VMEM, VMEM),
        compiler_params=PARAMS,
        name="term",
    )(core, pattern_ids[0], link_targets[0], live_counts, background, patterns[0])
    of_chip = keep + lax.ppermute(send, "c", [(0, 1), (1, 0)])
    parts = all_to_all(of_chip, ("y", "zl"))
    rows = local(rows_kernel, (8, 8, members), 1)(parts)
    own = all_to_all(rows, "zh")
    gram = local(gram_kernel, (64, 8, 128), 3)(own, counts_obs, obs_var)
    plane = local(share_kernel, (8, 8, 128), 1)(all_to_all(gram, SLAB))
    shared = local(share_kernel, (64, 8, 128), 1)(all_to_all(plane, "zh"))
    pieces = all_to_all(shared, SLAB)
    own_rows = states_dev // lax.axis_size("x")
    return pl.pallas_call(
        update_kernel,
        out_shape=jax.ShapeDtypeStruct((own_rows, members), BF16),
        grid_spec=pltpu.PrefetchScalarGridSpec(
            num_scalar_prefetch=2,
            grid=(1,),
            in_specs=[
                pl.BlockSpec((64, 8, 128), lambda i, link, live: (0, 0, 0)),
                pl.BlockSpec((own_rows, members), lambda i, link, live: (link[0], 0)),
            ],
            out_specs=pl.BlockSpec((own_rows, members), lambda i, link, live: (0, 0)),
        ),
        compiler_params=PARAMS,
        name="update",
    )(link, live_counts, pieces, background)


def solution(mesh):
    torus = Mesh(mesh.devices.reshape(4, 8, 2, 2, 4), ("y", "zh", "zl", "c", "x"))
    return jax.shard_map(
        per_device,
        mesh=torus,
        in_specs=(
            P(ORIG, None),
            P(ORIG),
            P("x", ORIG, None, None),
            P("x", ORIG, None),
            P("x", ORIG, None),
            P("x", ORIG),
            P("x", ORIG),
        ),
        out_specs=P((*ORIG, "x"), None),
        check_vma=False,
    )
```

```python
import jax
import jax.numpy as jnp
from jax import lax
from jax.experimental import pallas as pl
from jax.experimental.pallas import tpu as pltpu
from jax.sharding import Mesh
from jax.sharding import PartitionSpec as P

NLB = 8
NS_ITERS = 4
F32 = jnp.float32
BF16 = jnp.bfloat16
ORIG = ("y", "zh", "zl", "c")
SLAB = ("x", "y", "zl", "c")
VMEM = pl.BlockSpec(memory_space=pltpu.VMEM)
SMEM = pl.BlockSpec(memory_space=pltpu.SMEM)
HBM = pl.BlockSpec(memory_space=pltpu.HBM)
DEPTH = 8
WHOLE = pltpu.CompilerParams(vmem_limit_bytes=58 * 2**20)
PARAMS = pltpu.CompilerParams(vmem_limit_bytes=40 * 2**20)


def halves(a):
    high = a.astype(BF16)
    return high, (a - high.astype(F32)).astype(BF16)


def dot(a, b):
    return jnp.dot(a, b, preferred_element_type=F32)


def dot3(a, b):
    (ah, al), (bh, bl) = a, b
    return dot(ah, bh) + (dot(ah, bl) + dot(al, bh))


def term_kernel(
    core_ref, ids_hbm, targets_hbm, live_hbm, states_hbm, tiles_hbm, keep_ref, send_ref,
    ids_ref, targets_ref, live_ref, states_ref, tiles_ref, list_ref, sems,
):
    slots, _, blocks = ids_ref.shape
    stored, link_rows, block_rows = tiles_ref.shape
    states_dev, members = states_hbm.shape
    steps = list_ref.shape[0] // DEPTH
    empty = blocks * stored
    copies = [
        pltpu.make_async_copy(there, here, sems.at[i])
        for i, (there, here) in enumerate(
            (
                (ids_hbm, ids_ref),
                (targets_hbm, targets_ref),
                (live_hbm, live_ref),
                (states_hbm, states_ref.at[pl.ds(0, states_dev)]),
                (tiles_hbm, tiles_ref),
            )
        )
    ]
    for copy in copies:
        copy.start()
    for k in range(steps * DEPTH):
        list_ref[k] = empty
    keep_ref[...] = jnp.zeros_like(keep_ref)
    send_ref[...] = jnp.zeros_like(send_ref)
    states_ref[states_dev:, :] = jnp.zeros((block_rows, members), BF16)
    copies[0].wait()
    copies[1].wait()

    def bump(words, target):
        one = jnp.left_shift(jnp.int32(1), (target & 3) * 8)
        return words[0] + jnp.where(target < 4, one, 0), words[1] + jnp.where(target < 4, 0, one)

    def count(b, words):
        for t in range(slots):
            words = bump(words, targets_ref[t, 0, b])
        return words

    def put(b, words):
        for t in range(slots):
            target = targets_ref[t, 0, b]
            at = jnp.right_shift(jnp.where(target < 4, words[0], words[1]), (target & 3) * 8) & 255
            list_ref[at] = target * 1024 + (b * stored + ids_ref[t, 0, b])
            words = bump(words, target)
        return words

    none = jnp.int32(0)
    counted = lax.fori_loop(0, blocks, count, (none, none))
    first_step, starts = none, [none, none]
    for j in range(NLB):
        entries = jnp.right_shift(counted[j // 4], 8 * (j % 4)) & 255
        starts[j // 4] += jnp.left_shift(first_step * DEPTH, 8 * (j % 4))
        first_step += jnp.right_shift(entries + DEPTH - 1, DEPTH.bit_length() - 1)
    lax.fori_loop(0, blocks, put, tuple(starts))

    copies[2].wait()
    copies[3].wait()
    position = lax.broadcasted_iota(jnp.int32, (block_rows, members), 0)
    for b in range(blocks):
        rows = slice(b * block_rows, (b + 1) * block_rows)
        living = (position < live_ref[b]).astype(F32).astype(BF16)
        states_ref[rows, :] = states_ref[rows, :] * living
    copies[4].wait()

    def run(by_core):
        def step(i, carry):
            codes = [list_ref[i * DEPTH + k] for k in range(DEPTH)]
            tiles, states = [], []
            for code in codes:
                first = pl.multiple_of((jnp.right_shift(code, 5) & 31) * block_rows, block_rows)
                tiles.append(tiles_ref[code & 31])
                states.append(states_ref[pl.ds(first, block_rows), :])
            product = dot(jnp.concatenate(tiles, axis=1), jnp.concatenate(states, axis=0))
            target = jnp.right_shift(codes[0], 10)
            chunk = jnp.right_shift(target, 1) * 2
            for g in range(16):
                q, zl, c = g // 4, (g // 2) % 2, g % 2
                at = pl.ds(pl.multiple_of((target & 1) * 32 + q * 8, 8), 8)
                by_core[c][chunk + zl, at, :] += product[g * 8 : g * 8 + 8]
            return carry

        lax.fori_loop(0, steps, step, 0, unroll=steps)

    @pl.when(core_ref[0] == 0)
    def _():
        run((keep_ref, send_ref))

    @pl.when(core_ref[0] == 1)
    def _():
        run((send_ref, keep_ref))


def term(core, ids, targets, live, states, tiles):
    slots, _, blocks = ids.shape
    states_dev, members = states.shape
    steps = (slots * blocks + NLB * (DEPTH - 1)) // DEPTH
    half = jax.ShapeDtypeStruct((8, 64, members), F32)
    return pl.pallas_call(
        term_kernel,
        out_shape=(half, half),
        in_specs=[SMEM] + [HBM] * 5,
        out_specs=(VMEM, VMEM),
        scratch_shapes=[
            pltpu.SMEM(ids.shape, jnp.int32),
            pltpu.SMEM(ids.shape, jnp.int32),
            pltpu.SMEM(live.shape, jnp.int32),
            pltpu.VMEM((states_dev + tiles.shape[2], members), BF16),
            pltpu.VMEM(tiles.shape, BF16),
            pltpu.SMEM((steps * DEPTH,), jnp.int32),
            pltpu.SemaphoreType.DMA((5,)),
        ],
        compiler_params=WHOLE,
        name="term",
    )(core, ids, targets, live, states, tiles)


def as_column(ref):
    count = ref.shape[1]
    at = lambda dim: lax.broadcasted_iota(jnp.int32, (count, count), dim)
    return jnp.sum(jnp.where(at(0) == at(1), ref[...], 0.0), axis=1, keepdims=True)


def rows_kernel(parts_ref, counts_ref, var_ref, out_ref):
    total = jnp.sum(parts_ref[...], axis=0)
    rows = total.shape[0]
    out_ref[0:rows, :] = total[:, :128]
    out_ref[rows : 2 * rows, :] = total[:, 128:]
    lane = lax.broadcasted_iota(jnp.int32, (8, 128), 1)
    counts, variance = as_column(counts_ref), as_column(var_ref)
    out_ref[2 * rows : 2 * rows + 8, :] = jnp.where(lane == 0, counts, jnp.where(lane == 1, variance, 0.0))


def gram_kernel(parts_ref, out_ref):
    rows = (parts_ref.shape[1] - 8) // 2
    left = jnp.sum(parts_ref[:, 0:rows, :], axis=0)
    right = jnp.sum(parts_ref[:, rows : 2 * rows, :], axis=0)
    tail = parts_ref[:, 2 * rows :, :].reshape(rows, 128)
    counts, variance = tail[:, 0:1], tail[:, 1:2]
    mean = jnp.sum(left + right, axis=1, keepdims=True) * (1.0 / 256.0)
    spread = jnp.concatenate([left - mean, right - mean], axis=1)
    weights = 1.0 / variance
    forcing = jnp.sum(spread * (weights * (counts - mean)), axis=0, keepdims=True)
    gram = dot3(halves(spread.T), halves(spread * weights))
    out_ref[...] = jnp.zeros_like(out_ref)
    out_ref[0:16] = gram[:128, :128].reshape(16, 8, 128)
    out_ref[16:32] = gram[:128, 128:].reshape(16, 8, 128)
    out_ref[32:48] = gram[128:, 128:].reshape(16, 8, 128)
    out_ref[48, 0:1, :] = forcing[:, :128]
    out_ref[48, 1:2, :] = forcing[:, 128:]


def share_kernel(parts_ref, out_ref):
    total = jnp.sum(parts_ref[...], axis=0)
    out_ref[...] = jnp.broadcast_to(total[None], out_ref.shape)


def update_kernel(link_ref, live_ref, pieces_ref, states_hbm, out_ref, states_ref, sem):
    own_rows, members = states_ref.shape
    own = pl.ds(pl.multiple_of(link_ref[0] * own_rows, own_rows), own_rows)
    copy = pltpu.make_async_copy(states_hbm.at[own], states_ref, sem)
    copy.start()
    first = pieces_ref[0:16].reshape(128, 128)
    across = pieces_ref[16:32].reshape(128, 128)
    last = pieces_ref[32:48].reshape(128, 128)
    gram = jnp.concatenate(
        [jnp.concatenate([first, across], axis=1), jnp.concatenate([across.T, last], axis=1)], axis=0
    )
    forcing = jnp.concatenate([pieces_ref[48, 0:1, :], pieces_ref[48, 1:2, :]], axis=1)
    at = lambda dim: lax.broadcasted_iota(jnp.int32, (members, members), dim)
    identity = jnp.where(at(0) == at(1), 1.0, 0.0).astype(F32)
    system = identity + gram * (1.0 / (members - 1.0))
    bound = jnp.max(jnp.sum(jnp.abs(system), axis=0, keepdims=True), axis=1, keepdims=True)
    root = system * (1.0 / bound)
    inverse = identity
    for sweep in range(NS_ITERS):
        if sweep == 0:
            middle = 1.5 * identity - 0.5 * root
            inverse = middle
        else:
            middle = 1.5 * identity - 0.5 * dot3(halves(inverse), halves(root))
        middle_halves = halves(middle)
        if sweep > 0:
            inverse = dot3(middle_halves, halves(inverse))
        if sweep < NS_ITERS - 1:
            root = dot3(halves(root), middle_halves)
    inner = dot3(halves(jnp.broadcast_to(forcing, (8, members))), halves(inverse))[0:1]
    mean_weights = jnp.sum(inverse * inner, axis=1, keepdims=True) * (1.0 / (bound * (members - 1.0)))
    transform = inverse * lax.rsqrt(bound) + mean_weights
    transform += (1.0 - jnp.sum(transform, axis=0, keepdims=True)) * (1.0 / members)
    high, low = halves(transform)
    copy.wait()
    own_blocks = own_rows // 128
    position = lax.broadcasted_iota(jnp.int32, (128, members), 0)
    for k in range(own_blocks):
        rows = slice(k * 128, k * 128 + 128)
        states = states_ref[rows, :]
        updated = dot(states, high) + dot(states, low)
        live = live_ref[link_ref[0] * own_blocks + k]
        out_ref[rows, :] = jnp.where(position < live, updated, states.astype(F32)).astype(BF16)


def all_to_all(x, axes):
    return lax.all_to_all(x, axes, split_axis=0, concat_axis=0, tiled=True)


def local(kernel, shape, operands):
    return pl.pallas_call(
        kernel,
        out_shape=jax.ShapeDtypeStruct(shape, F32),
        in_specs=[VMEM] * operands,
        out_specs=VMEM,
        compiler_params=PARAMS,
        name=kernel.__name__,
    )


def per_device(background, live_counts, patterns, pattern_ids, link_targets, counts_obs, obs_var):
    states_dev, members = background.shape
    core = lax.axis_index("c").astype(jnp.int32).reshape(1)
    link = lax.axis_index("x").astype(jnp.int32).reshape(1)
    ids, targets = (jnp.transpose(a, (2, 0, 1)) for a in (pattern_ids, link_targets))
    keep, send = term(core, ids, targets, live_counts, background, patterns[0])
    of_chip = keep + lax.ppermute(send, "c", [(0, 1), (1, 0)])
    parts = all_to_all(of_chip, ("y", "zl"))
    own = local(rows_kernel, (136, 128), 3)(parts, counts_obs, obs_var)
    column = lax.all_gather(own, "zh")
    gram = local(gram_kernel, (64, 8, 128), 1)(column)
    shared = local(share_kernel, (64, 8, 128), 1)(all_to_all(gram, SLAB))
    pieces = all_to_all(shared, SLAB)
    own_rows = states_dev // lax.axis_size("x")
    return pl.pallas_call(
        update_kernel,
        out_shape=jax.ShapeDtypeStruct((own_rows, members), BF16),
        in_specs=[SMEM, SMEM, VMEM, HBM],
        out_specs=VMEM,
        scratch_shapes=[pltpu.VMEM((own_rows, members), BF16), pltpu.SemaphoreType.DMA],
        compiler_params=PARAMS,
        name="update",
    )(link, live_counts, pieces, background)


def solution(mesh):
    torus = Mesh(mesh.devices.reshape(4, 8, 2, 2, 4), ("y", "zh", "zl", "c", "x"))
    return jax.shard_map(
        per_device,
        mesh=torus,
        in_specs=(
            P(ORIG, None),
            P(ORIG),
            P("x", ORIG, None, None),
            P("x", ORIG, None),
            P("x", ORIG, None),
            P("x", ORIG),
            P("x", ORIG),
        ),
        out_specs=P((*ORIG, "x"), None),
        check_vma=False,
    )
```

```python
import jax
import jax.numpy as jnp
from jax import lax
from jax.experimental import pallas as pl
from jax.experimental.pallas import tpu as pltpu
from jax.sharding import Mesh
from jax.sharding import PartitionSpec as P

NLB = 8
NS_ITERS = 4
F32 = jnp.float32
BF16 = jnp.bfloat16
ORIG = ("y", "zq", "zp", "zl", "c")
SLAB = ("x", "y", "zl", "c")
VMEM = pl.BlockSpec(memory_space=pltpu.VMEM)
SMEM = pl.BlockSpec(memory_space=pltpu.SMEM)
HBM = pl.BlockSpec(memory_space=pltpu.HBM)
DEPTH = 8
WHOLE = pltpu.CompilerParams(vmem_limit_bytes=58 * 2**20)
PARAMS = pltpu.CompilerParams(vmem_limit_bytes=40 * 2**20)


def halves(a):
    high = a.astype(BF16)
    return high, (a - high.astype(F32)).astype(BF16)


def dot(a, b):
    return jnp.dot(a, b, preferred_element_type=F32)


def dot3(a, b):
    (ah, al), (bh, bl) = a, b
    return dot(ah, bh) + (dot(ah, bl) + dot(al, bh))


def term_kernel(
    core_ref, ids_hbm, targets_hbm, live_hbm, states_hbm, tiles_hbm, keep_ref, send_ref,
    ids_ref, targets_ref, live_ref, states_ref, tiles_ref, list_ref, sems,
):
    slots, _, blocks = ids_ref.shape
    stored, link_rows, block_rows = tiles_ref.shape
    states_dev, members = states_hbm.shape
    steps = list_ref.shape[0] // DEPTH
    empty = blocks * stored
    copies = [
        pltpu.make_async_copy(there, here, sems.at[i])
        for i, (there, here) in enumerate(
            (
                (ids_hbm, ids_ref),
                (targets_hbm, targets_ref),
                (live_hbm, live_ref),
                (states_hbm, states_ref.at[pl.ds(0, states_dev)]),
                (tiles_hbm, tiles_ref),
            )
        )
    ]
    for copy in copies:
        copy.start()
    for k in range(steps * DEPTH):
        list_ref[k] = empty
    keep_ref[...] = jnp.zeros_like(keep_ref)
    send_ref[...] = jnp.zeros_like(send_ref)
    states_ref[states_dev:, :] = jnp.zeros((block_rows, members), BF16)
    copies[0].wait()
    copies[1].wait()

    def bump(words, target):
        one = jnp.left_shift(jnp.int32(1), (target & 3) * 8)
        return words[0] + jnp.where(target < 4, one, 0), words[1] + jnp.where(target < 4, 0, one)

    def count(b, words):
        for t in range(slots):
            words = bump(words, targets_ref[t, 0, b])
        return words

    def put(b, words):
        for t in range(slots):
            target = targets_ref[t, 0, b]
            at = jnp.right_shift(jnp.where(target < 4, words[0], words[1]), (target & 3) * 8) & 255
            list_ref[at] = target * 1024 + (b * stored + ids_ref[t, 0, b])
            words = bump(words, target)
        return words

    none = jnp.int32(0)
    counted = lax.fori_loop(0, blocks, count, (none, none))
    first_step, starts = none, [none, none]
    for j in range(NLB):
        entries = jnp.right_shift(counted[j // 4], 8 * (j % 4)) & 255
        starts[j // 4] += jnp.left_shift(first_step * DEPTH, 8 * (j % 4))
        first_step += jnp.right_shift(entries + DEPTH - 1, DEPTH.bit_length() - 1)
    lax.fori_loop(0, blocks, put, tuple(starts))

    copies[2].wait()
    copies[3].wait()
    position = lax.broadcasted_iota(jnp.int32, (block_rows, members), 0)
    for b in range(blocks):
        rows = slice(b * block_rows, (b + 1) * block_rows)
        living = (position < live_ref[b]).astype(F32).astype(BF16)
        states_ref[rows, :] = states_ref[rows, :] * living
    copies[4].wait()

    def run(by_core):
        def step(i, carry):
            codes = [list_ref[i * DEPTH + k] for k in range(DEPTH)]
            tiles, states = [], []
            for code in codes:
                first = pl.multiple_of((jnp.right_shift(code, 5) & 31) * block_rows, block_rows)
                tiles.append(tiles_ref[code & 31])
                states.append(states_ref[pl.ds(first, block_rows), :])
            product = dot(jnp.concatenate(tiles, axis=1), jnp.concatenate(states, axis=0))
            target = jnp.right_shift(codes[0], 10)
            chunk = jnp.right_shift(target, 1) * 2
            for g in range(16):
                q, zl, c = g // 4, (g // 2) % 2, g % 2
                at = pl.ds(pl.multiple_of((target & 1) * 32 + q * 8, 8), 8)
                by_core[c][chunk + zl, at, :] += product[g * 8 : g * 8 + 8]
            return carry

        lax.fori_loop(0, steps, step, 0, unroll=steps)

    @pl.when(core_ref[0] == 0)
    def _():
        run((keep_ref, send_ref))

    @pl.when(core_ref[0] == 1)
    def _():
        run((send_ref, keep_ref))


def term(core, ids, targets, live, states, tiles):
    slots, _, blocks = ids.shape
    states_dev, members = states.shape
    steps = (slots * blocks + NLB * (DEPTH - 1)) // DEPTH
    half = jax.ShapeDtypeStruct((8, 64, members), F32)
    return pl.pallas_call(
        term_kernel,
        out_shape=(half, half),
        in_specs=[SMEM] + [HBM] * 5,
        out_specs=(VMEM, VMEM),
        scratch_shapes=[
            pltpu.SMEM(ids.shape, jnp.int32),
            pltpu.SMEM(ids.shape, jnp.int32),
            pltpu.SMEM(live.shape, jnp.int32),
            pltpu.VMEM((states_dev + tiles.shape[2], members), BF16),
            pltpu.VMEM(tiles.shape, BF16),
            pltpu.SMEM((steps * DEPTH,), jnp.int32),
            pltpu.SemaphoreType.DMA((5,)),
        ],
        compiler_params=WHOLE,
        name="term",
    )(core, ids, targets, live, states, tiles)


def as_column(ref):
    count = ref.shape[1]
    at = lambda dim: lax.broadcasted_iota(jnp.int32, (count, count), dim)
    return jnp.sum(jnp.where(at(0) == at(1), ref[...], 0.0), axis=1, keepdims=True)


def rows_kernel(pair_ref, parts_ref, counts_ref, var_ref, out_ref):
    total = jnp.sum(parts_ref[...], axis=0)
    rows = total.shape[0]
    out_ref[0:rows, :] = total[:, :128]
    out_ref[rows : 2 * rows, :] = total[:, 128:]
    lane = lax.broadcasted_iota(jnp.int32, (8, 128), 1) - 2 * pair_ref[0]
    counts, variance = as_column(counts_ref), as_column(var_ref)
    out_ref[2 * rows : 2 * rows + 8, :] = jnp.where(lane == 0, counts, jnp.where(lane == 1, variance, 0.0))


def gram_kernel(core_ref, parts_ref, out_ref):
    rows = (parts_ref.shape[1] - 8) // 2
    quads = parts_ref.shape[0] // 2

    def both(first, count):
        return jnp.concatenate(
            [sum(parts_ref[2 * k + c, first : first + count, :] for k in range(quads)) for c in range(2)], axis=0
        )

    left, right = both(0, rows), both(rows, rows)
    tails = [parts_ref[2 * k + c, 2 * rows : 2 * rows + 8, :] for c in range(2) for k in range(quads)]
    column = lambda at: jnp.concatenate([t[:, 2 * p + at : 2 * p + at + 1] for t in tails for p in range(2)], axis=0)
    counts, variance = column(0), column(1)
    mean = jnp.sum(left + right, axis=1, keepdims=True) * (1.0 / 256.0)
    left, right = left - mean, right - mean
    weights = 1.0 / variance
    weighted = weights * (counts - mean)
    mine = core_ref[0] == 0
    own = jnp.where(mine, left, right)
    half = jnp.where(mine, left[:, :64], left[:, 64:])
    out_ref[0:16] = dot3(halves(own.T), halves(own * weights)).reshape(16, 8, 128)
    out_ref[16:24] = dot3(halves(half.T), halves(right * weights)).reshape(8, 8, 128)
    forcing = [jnp.sum(part * weighted, axis=0, keepdims=True) for part in (left, right)]
    out_ref[24] = jnp.concatenate([*forcing, jnp.zeros((6, 128), F32)], axis=0)
    out_ref[25:] = jnp.zeros((out_ref.shape[0] - 25, 8, 128), F32)


def share_kernel(parts_ref, out_ref):
    total = jnp.sum(parts_ref[...], axis=0)
    out_ref[...] = jnp.broadcast_to(total[None], out_ref.shape)


def update_kernel(link_ref, live_ref, pieces_ref, states_hbm, out_ref, states_ref, sem):
    own_rows, members = states_ref.shape
    own = pl.ds(pl.multiple_of(link_ref[0] * own_rows, own_rows), own_rows)
    copy = pltpu.make_async_copy(states_hbm.at[own], states_ref, sem)
    copy.start()
    by_core = pieces_ref[...].reshape(pieces_ref.shape[0] // 2, 2, 8, 128)
    first = by_core[0:16, 0].reshape(128, 128)
    last = by_core[0:16, 1].reshape(128, 128)
    across = jnp.concatenate([by_core[16:24, c].reshape(64, 128) for c in range(2)], axis=0)
    gram = jnp.concatenate(
        [jnp.concatenate([first, across], axis=1), jnp.concatenate([across.T, last], axis=1)], axis=0
    )
    forcing = jnp.concatenate([by_core[24, 0, 0:1], by_core[24, 0, 1:2]], axis=1)
    at = lambda dim: lax.broadcasted_iota(jnp.int32, (members, members), dim)
    identity = jnp.where(at(0) == at(1), 1.0, 0.0).astype(F32)
    system = identity + gram * (1.0 / (members - 1.0))
    bound = jnp.max(jnp.sum(jnp.abs(system), axis=0, keepdims=True), axis=1, keepdims=True)
    root = system * (1.0 / bound)
    inverse = identity
    for sweep in range(NS_ITERS):
        if sweep == 0:
            middle = 1.5 * identity - 0.5 * root
            inverse = middle
        else:
            middle = 1.5 * identity - 0.5 * dot3(halves(inverse), halves(root))
        middle_halves = halves(middle)
        if sweep > 0:
            inverse = dot3(middle_halves, halves(inverse))
        if sweep < NS_ITERS - 1:
            root = dot3(halves(root), middle_halves)
    inner = dot3(halves(jnp.broadcast_to(forcing, (8, members))), halves(inverse))[0:1]
    mean_weights = jnp.sum(inverse * inner, axis=1, keepdims=True) * (1.0 / (bound * (members - 1.0)))
    transform = inverse * lax.rsqrt(bound) + mean_weights
    transform += (1.0 - jnp.sum(transform, axis=0, keepdims=True)) * (1.0 / members)
    high, low = halves(transform)
    copy.wait()
    own_blocks = own_rows // 128
    position = lax.broadcasted_iota(jnp.int32, (128, members), 0)
    for k in range(own_blocks):
        rows = slice(k * 128, k * 128 + 128)
        states = states_ref[rows, :]
        updated = dot(states, high) + dot(states, low)
        live = live_ref[link_ref[0] * own_blocks + k]
        out_ref[rows, :] = jnp.where(position < live, updated, states.astype(F32)).astype(BF16)


def all_to_all(x, axes):
    return lax.all_to_all(x, axes, split_axis=0, concat_axis=0, tiled=True)


def local(kernel, shape, operands, scalars=0):
    return pl.pallas_call(
        kernel,
        out_shape=jax.ShapeDtypeStruct(shape, F32),
        in_specs=[SMEM] * scalars + [VMEM] * operands,
        out_specs=VMEM,
        compiler_params=PARAMS,
        name=kernel.__name__,
    )


def per_device(background, live_counts, patterns, pattern_ids, link_targets, counts_obs, obs_var):
    states_dev, members = background.shape
    core, link, pair = (lax.axis_index(axis).astype(jnp.int32).reshape(1) for axis in ("c", "x", "zp"))
    ids, targets = (jnp.transpose(a, (2, 0, 1)) for a in (pattern_ids, link_targets))
    keep, send = term(core, ids, targets, live_counts, background, patterns[0])
    of_chip = keep + lax.ppermute(send, "c", [(0, 1), (1, 0)])
    parts = all_to_all(of_chip, ("y", "zl"))
    own = local(rows_kernel, (136, 128), 3, 1)(pair, parts, counts_obs, obs_var)
    own += lax.ppermute(own, "zp", [(0, 1), (1, 0)])
    column = lax.all_gather(own, ("zq", "c"))
    gram = local(gram_kernel, (32, 8, 128), 1, 1)(core, column)
    shared = local(share_kernel, (64, 8, 128), 1)(all_to_all(gram, ("x", "y", "zl")))
    pieces = all_to_all(shared, SLAB)
    own_rows = states_dev // lax.axis_size("x")
    return pl.pallas_call(
        update_kernel,
        out_shape=jax.ShapeDtypeStruct((own_rows, members), BF16),
        in_specs=[SMEM, SMEM, VMEM, HBM],
        out_specs=VMEM,
        scratch_shapes=[pltpu.VMEM((own_rows, members), BF16), pltpu.SemaphoreType.DMA],
        compiler_params=PARAMS,
        name="update",
    )(link, live_counts, pieces, background)


def solution(mesh):
    torus = Mesh(mesh.devices.reshape(4, 4, 2, 2, 2, 4), ("y", "zq", "zp", "zl", "c", "x"))
    return jax.shard_map(
        per_device,
        mesh=torus,
        in_specs=(
            P(ORIG, None),
            P(ORIG),
            P("x", ORIG, None, None),
            P("x", ORIG, None),
            P("x", ORIG, None),
            P("x", ORIG),
            P("x", ORIG),
        ),
        out_specs=P((*ORIG, "x"), None),
        check_vma=False,
    )
```

```python
import jax
import jax.numpy as jnp
from jax import lax
from jax.experimental import pallas as pl
from jax.experimental.pallas import tpu as pltpu
from jax.sharding import Mesh
from jax.sharding import PartitionSpec as P

NLB = 8
NS_ITERS = 4
F32 = jnp.float32
BF16 = jnp.bfloat16
ORIG = ("y", "zq", "zp", "zl", "c")
SLAB = ("x", "y", "zl", "c")
VMEM = pl.BlockSpec(memory_space=pltpu.VMEM)
SMEM = pl.BlockSpec(memory_space=pltpu.SMEM)
HBM = pl.BlockSpec(memory_space=pltpu.HBM)
DEPTH = 8
WHOLE = pltpu.CompilerParams(vmem_limit_bytes=58 * 2**20)
PARAMS = pltpu.CompilerParams(vmem_limit_bytes=40 * 2**20)


def halves(a):
    high = a.astype(BF16)
    return high, (a - high.astype(F32)).astype(BF16)


def dot(a, b):
    return jnp.dot(a, b, preferred_element_type=F32)


def dot3(a, b):
    (ah, al), (bh, bl) = a, b
    return dot(ah, bh) + (dot(ah, bl) + dot(al, bh))


def link_of(place_ref):
    return place_ref[0] & 3


def core_of(place_ref):
    return jnp.right_shift(place_ref[0], 2) & 1


def pair_of(place_ref):
    return jnp.right_shift(place_ref[0], 4) & 1


def term_kernel(
    place_ref, ids_hbm, targets_hbm, live_hbm, states_hbm, tiles_hbm, keep_ref, send_ref,
    ids_ref, targets_ref, live_ref, states_ref, tiles_ref, list_ref, sems,
):
    slots, _, blocks = ids_ref.shape
    stored, link_rows, block_rows = tiles_ref.shape
    states_dev, members = states_hbm.shape
    steps = list_ref.shape[0] // DEPTH
    empty = blocks * stored
    copies = [
        pltpu.make_async_copy(there, here, sems.at[i])
        for i, (there, here) in enumerate(
            (
                (ids_hbm, ids_ref),
                (targets_hbm, targets_ref),
                (live_hbm, live_ref),
                (states_hbm, states_ref.at[pl.ds(0, states_dev)]),
                (tiles_hbm, tiles_ref),
            )
        )
    ]
    for copy in copies:
        copy.start()
    for k in range(steps * DEPTH):
        list_ref[k] = empty
    keep_ref[...] = jnp.zeros_like(keep_ref)
    send_ref[...] = jnp.zeros_like(send_ref)
    states_ref[states_dev:, :] = jnp.zeros((block_rows, members), BF16)
    copies[0].wait()
    copies[1].wait()

    def bump(words, target):
        one = jnp.left_shift(jnp.int32(1), (target & 3) * 8)
        return words[0] + jnp.where(target < 4, one, 0), words[1] + jnp.where(target < 4, 0, one)

    def count(b, words):
        for t in range(slots):
            words = bump(words, targets_ref[t, 0, b])
        return words

    def put(b, words):
        for t in range(slots):
            target = targets_ref[t, 0, b]
            at = jnp.right_shift(jnp.where(target < 4, words[0], words[1]), (target & 3) * 8) & 255
            list_ref[at] = target * 1024 + (b * stored + ids_ref[t, 0, b])
            words = bump(words, target)
        return words

    none = jnp.int32(0)
    counted = lax.fori_loop(0, blocks, count, (none, none))
    first_step, starts = none, [none, none]
    for j in range(NLB):
        entries = jnp.right_shift(counted[j // 4], 8 * (j % 4)) & 255
        starts[j // 4] += jnp.left_shift(first_step * DEPTH, 8 * (j % 4))
        first_step += jnp.right_shift(entries + DEPTH - 1, DEPTH.bit_length() - 1)
    lax.fori_loop(0, blocks, put, tuple(starts))

    copies[2].wait()
    copies[3].wait()
    position = lax.broadcasted_iota(jnp.int32, (block_rows, members), 0)
    for b in range(blocks):
        rows = slice(b * block_rows, (b + 1) * block_rows)
        living = (position < live_ref[b]).astype(F32).astype(BF16)
        states_ref[rows, :] = states_ref[rows, :] * living
    copies[4].wait()

    def run(by_core):
        def step(i, carry):
            codes = [list_ref[i * DEPTH + k] for k in range(DEPTH)]
            tiles, states = [], []
            for code in codes:
                first = pl.multiple_of((jnp.right_shift(code, 5) & 31) * block_rows, block_rows)
                tiles.append(tiles_ref[code & 31])
                states.append(states_ref[pl.ds(first, block_rows), :])
            product = dot(jnp.concatenate(tiles, axis=1), jnp.concatenate(states, axis=0))
            target = jnp.right_shift(codes[0], 10)
            chunk = jnp.right_shift(target, 1) * 2
            for g in range(16):
                q, zl, c = g // 4, (g // 2) % 2, g % 2
                at = pl.ds(pl.multiple_of((target & 1) * 32 + q * 8, 8), 8)
                by_core[c][chunk + zl, at, :] += product[g * 8 : g * 8 + 8]
            return carry

        lax.fori_loop(0, steps, step, 0, unroll=steps)

    @pl.when(core_of(place_ref) == 0)
    def _():
        run((keep_ref, send_ref))

    @pl.when(core_of(place_ref) == 1)
    def _():
        run((send_ref, keep_ref))


def term(place, ids, targets, live, states, tiles):
    slots, _, blocks = ids.shape
    states_dev, members = states.shape
    steps = (slots * blocks + NLB * (DEPTH - 1)) // DEPTH
    half = jax.ShapeDtypeStruct((8, 64, members), F32)
    return pl.pallas_call(
        term_kernel,
        out_shape=(half, half),
        in_specs=[SMEM] + [HBM] * 5,
        out_specs=(VMEM, VMEM),
        scratch_shapes=[
            pltpu.SMEM(ids.shape, jnp.int32),
            pltpu.SMEM(ids.shape, jnp.int32),
            pltpu.SMEM(live.shape, jnp.int32),
            pltpu.VMEM((states_dev + tiles.shape[2], members), BF16),
            pltpu.VMEM(tiles.shape, BF16),
            pltpu.SMEM((steps * DEPTH,), jnp.int32),
            pltpu.SemaphoreType.DMA((5,)),
        ],
        compiler_params=WHOLE,
        name="term",
    )(place, ids, targets, live, states, tiles)


def as_column(ref):
    count = ref.shape[1]
    at = lambda dim: lax.broadcasted_iota(jnp.int32, (count, count), dim)
    return jnp.sum(jnp.where(at(0) == at(1), ref[...], 0.0), axis=1, keepdims=True)


def add_kernel(a_ref, b_ref, out_ref):
    out_ref[...] = a_ref[...] + b_ref[...]


def rows_kernel(place_ref, parts_ref, counts_ref, var_ref, keep_ref, send_ref):
    total = jnp.sum(parts_ref[...], axis=0)
    rows, members = total.shape
    by_pair = total.reshape(rows // 16, 2, 8, members)
    first, second = (by_pair[:, p].reshape(rows // 2, members) for p in range(2))
    mine = pair_of(place_ref) == 0
    lane = lax.broadcasted_iota(jnp.int32, (8, 128), 1)
    counts, variance = as_column(counts_ref), as_column(var_ref)
    tail = jnp.where(lane == 0, counts, jnp.where(lane == 1, variance, 0.0))
    for ref, at, below in ((keep_ref, mine, tail), (send_ref, jnp.logical_not(mine), jnp.zeros_like(tail))):
        chosen = jnp.where(at, first, second)
        ref[0 : rows // 2, :] = chosen[:, :128]
        ref[rows // 2 : rows, :] = chosen[:, 128:]
        ref[rows:, :] = below


def gram_kernel(place_ref, parts_ref, out_ref):
    rows = (parts_ref.shape[1] - 8) // 2
    quads = parts_ref.shape[0] // 4
    groups = [[(2 * k + p) * 2 + c for k in range(quads)] for c in range(2) for p in range(2)]

    def whole(first):
        return jnp.concatenate([sum(parts_ref[m, first : first + rows, :] for m in g) for g in groups], axis=0)

    left, right = whole(0), whole(rows)
    tails = jnp.concatenate([parts_ref[m, 2 * rows :, :] for g in groups for m in g], axis=0)
    counts, variance = tails[:, 0:1], tails[:, 1:2]
    mean = jnp.sum(left + right, axis=1, keepdims=True) * (1.0 / 256.0)
    left, right = left - mean, right - mean
    weights = 1.0 / variance
    weighted = weights * (counts - mean)
    mine = core_of(place_ref) == 0
    own = jnp.where(mine, left, right)
    half = jnp.where(mine, left[:, :64], left[:, 64:])
    out_ref[0:16] = dot3(halves(own.T), halves(own * weights)).reshape(16, 8, 128)
    out_ref[16:24] = dot3(halves(half.T), halves(right * weights)).reshape(8, 8, 128)
    forcing = [jnp.sum(part * weighted, axis=0, keepdims=True) for part in (left, right)]
    out_ref[24] = jnp.concatenate([*forcing, jnp.zeros((6, 128), F32)], axis=0)
    out_ref[25:] = jnp.zeros((out_ref.shape[0] - 25, 8, 128), F32)


def share_kernel(parts_ref, out_ref):
    total = jnp.sum(parts_ref[...], axis=0)
    out_ref[...] = jnp.broadcast_to(total[None], out_ref.shape)


def update_kernel(place_ref, live_ref, pieces_ref, states_hbm, out_ref, states_ref, sem):
    own_rows, members = states_ref.shape
    own = pl.ds(pl.multiple_of(link_of(place_ref) * own_rows, own_rows), own_rows)
    copy = pltpu.make_async_copy(states_hbm.at[own], states_ref, sem)
    copy.start()
    by_core = pieces_ref[...].reshape(pieces_ref.shape[0] // 2, 2, 8, 128)
    first = by_core[0:16, 0].reshape(128, 128)
    last = by_core[0:16, 1].reshape(128, 128)
    across = jnp.concatenate([by_core[16:24, c].reshape(64, 128) for c in range(2)], axis=0)
    gram = jnp.concatenate(
        [jnp.concatenate([first, across], axis=1), jnp.concatenate([across.T, last], axis=1)], axis=0
    )
    forcing = jnp.concatenate([by_core[24, 0, 0:1], by_core[24, 0, 1:2]], axis=1)
    at = lambda dim: lax.broadcasted_iota(jnp.int32, (members, members), dim)
    identity = jnp.where(at(0) == at(1), 1.0, 0.0).astype(F32)
    system = identity + gram * (1.0 / (members - 1.0))
    bound = jnp.max(jnp.sum(jnp.abs(system), axis=0, keepdims=True), axis=1, keepdims=True)
    root = system * (1.0 / bound)
    inverse = identity
    for sweep in range(NS_ITERS):
        if sweep == 0:
            middle = 1.5 * identity - 0.5 * root
            inverse = middle
        else:
            middle = 1.5 * identity - 0.5 * dot3(halves(inverse), halves(root))
        middle_halves = halves(middle)
        if sweep > 0:
            inverse = dot3(middle_halves, halves(inverse))
        if sweep < NS_ITERS - 1:
            root = dot3(halves(root), middle_halves)
    inner = dot3(halves(jnp.broadcast_to(forcing, (8, members))), halves(inverse))[0:1]
    mean_weights = jnp.sum(inverse * inner, axis=1, keepdims=True) * (1.0 / (bound * (members - 1.0)))
    transform = inverse * lax.rsqrt(bound) + mean_weights
    transform += (1.0 - jnp.sum(transform, axis=0, keepdims=True)) * (1.0 / members)
    high, low = halves(transform)
    copy.wait()
    own_blocks = own_rows // 128
    position = lax.broadcasted_iota(jnp.int32, (128, members), 0)
    for k in range(own_blocks):
        rows = slice(k * 128, k * 128 + 128)
        states = states_ref[rows, :]
        updated = dot(states, high) + dot(states, low)
        live = live_ref[link_of(place_ref) * own_blocks + k]
        out_ref[rows, :] = jnp.where(position < live, updated, states.astype(F32)).astype(BF16)


def all_to_all(x, axes):
    return lax.all_to_all(x, axes, split_axis=0, concat_axis=0, tiled=True)


def local(kernel, shape, operands, scalars=0):
    return pl.pallas_call(
        kernel,
        out_shape=jax.ShapeDtypeStruct(shape, F32),
        in_specs=[SMEM] * scalars + [VMEM] * operands,
        out_specs=VMEM,
        compiler_params=PARAMS,
        name=kernel.__name__,
    )


def per_device(background, live_counts, patterns, pattern_ids, link_targets, counts_obs, obs_var):
    states_dev, members = background.shape
    place = lax.axis_index(("zp", "zl", "c", "x")).astype(jnp.int32).reshape(1)
    ids, targets = (jnp.transpose(a, (2, 0, 1)) for a in (pattern_ids, link_targets))
    keep, send = term(place, ids, targets, live_counts, background, patterns[0])
    of_chip = local(add_kernel, keep.shape, 2)(keep, lax.ppermute(send, "c", [(0, 1), (1, 0)]))
    parts = all_to_all(of_chip, ("y", "zl"))
    own, other = pl.pallas_call(
        rows_kernel,
        out_shape=(jax.ShapeDtypeStruct((72, 128), F32),) * 2,
        in_specs=[SMEM, VMEM, VMEM, VMEM],
        out_specs=(VMEM, VMEM),
        compiler_params=PARAMS,
        name="rows",
    )(place, parts, counts_obs, obs_var)
    own += lax.ppermute(other, "zp", [(0, 1), (1, 0)])
    column = lax.all_gather(own, ("zq", "zp", "c"))
    gram = local(gram_kernel, (32, 8, 128), 1, 1)(place, column)
    shared = local(share_kernel, (64, 8, 128), 1)(all_to_all(gram, ("x", "y", "zl")))
    pieces = all_to_all(shared, SLAB)
    own_rows = states_dev // lax.axis_size("x")
    return pl.pallas_call(
        update_kernel,
        out_shape=jax.ShapeDtypeStruct((own_rows, members), BF16),
        in_specs=[SMEM, SMEM, VMEM, HBM],
        out_specs=VMEM,
        scratch_shapes=[pltpu.VMEM((own_rows, members), BF16), pltpu.SemaphoreType.DMA],
        compiler_params=PARAMS,
        name="update",
    )(place, live_counts, pieces, background)


def solution(mesh):
    torus = Mesh(mesh.devices.reshape(4, 4, 2, 2, 2, 4), ("y", "zq", "zp", "zl", "c", "x"))
    return jax.shard_map(
        per_device,
        mesh=torus,
        in_specs=(
            P(ORIG, None),
            P(ORIG),
            P("x", ORIG, None, None),
            P("x", ORIG, None),
            P("x", ORIG, None),
            P("x", ORIG),
            P("x", ORIG),
        ),
        out_specs=P((*ORIG, "x"), None),
        check_vma=False,
    )
```

```python
import jax
import jax.numpy as jnp
from jax import lax
from jax.experimental import pallas as pl
from jax.experimental.pallas import tpu as pltpu
from jax.sharding import Mesh
from jax.sharding import PartitionSpec as P

NLB = 8
NS_ITERS = 4
F32 = jnp.float32
BF16 = jnp.bfloat16
ORIG = ("y", "zq", "zp", "zl", "c")
SLAB = ("x", "y", "zl", "c")
VMEM = pl.BlockSpec(memory_space=pltpu.VMEM)
SMEM = pl.BlockSpec(memory_space=pltpu.SMEM)
HBM = pl.BlockSpec(memory_space=pltpu.HBM)
DEPTH = 8
WHOLE = pltpu.CompilerParams(vmem_limit_bytes=58 * 2**20)
PARAMS = pltpu.CompilerParams(vmem_limit_bytes=40 * 2**20)


def halves(a):
    high = a.astype(BF16)
    return high, (a - high.astype(F32)).astype(BF16)


def dot(a, b):
    return jnp.dot(a, b, preferred_element_type=F32)


def dot3(a, b):
    (ah, al), (bh, bl) = a, b
    return dot(ah, bh) + (dot(ah, bl) + dot(al, bh))


def link_of(place_ref):
    return place_ref[0] & 3


def core_of(place_ref):
    return jnp.right_shift(place_ref[0], 2) & 1


def pair_of(place_ref):
    return jnp.right_shift(place_ref[0], 4) & 1


def term_kernel(
    place_ref, ids_hbm, targets_hbm, live_hbm, states_hbm, tiles_hbm, keep_ref, send_ref,
    ids_ref, targets_ref, live_ref, states_ref, tiles_ref, spread_ref, next_ref, list_ref, sems,
):
    slots, _, blocks = ids_ref.shape
    stored, link_rows, block_rows = tiles_ref.shape
    states_dev, members = states_hbm.shape
    steps = list_ref.shape[0] // DEPTH
    empty = blocks * stored
    copies = [
        pltpu.make_async_copy(there, here, sems.at[i])
        for i, (there, here) in enumerate(
            (
                (ids_hbm, ids_ref),
                (targets_hbm, targets_ref),
                (live_hbm, live_ref),
                (states_hbm, states_ref.at[pl.ds(0, states_dev)]),
                (tiles_hbm, tiles_ref),
                (targets_hbm, spread_ref),
            )
        )
    ]
    for copy in copies:
        copy.start()
    for k in range(steps * DEPTH):
        list_ref[k] = empty
    keep_ref[...] = jnp.zeros_like(keep_ref)
    send_ref[...] = jnp.zeros_like(send_ref)
    states_ref[states_dev:, :] = jnp.zeros((block_rows, members), BF16)
    copies[5].wait()
    spread = spread_ref[...]
    first_step = jnp.int32(0)
    for j in range(NLB):
        entries = jnp.sum(jnp.where(spread == j, 1.0, 0.0)).astype(jnp.int32)
        next_ref[j] = first_step * DEPTH
        first_step += jnp.right_shift(entries + DEPTH - 1, DEPTH.bit_length() - 1)
    copies[0].wait()
    copies[1].wait()

    def put(b, carry):
        for t in range(slots):
            target = targets_ref[t, 0, b]
            at = next_ref[target]
            list_ref[at] = target * 1024 + (b * stored + ids_ref[t, 0, b])
            next_ref[target] = at + 1
        return carry

    lax.fori_loop(0, blocks, put, 0, unroll=4)

    copies[2].wait()
    copies[3].wait()
    position = lax.broadcasted_iota(jnp.int32, (block_rows, members), 0)
    for b in range(blocks):
        rows = slice(b * block_rows, (b + 1) * block_rows)
        living = (position < live_ref[b]).astype(F32).astype(BF16)
        states_ref[rows, :] = states_ref[rows, :] * living
    copies[4].wait()

    def run(by_core):
        def step(i, carry):
            codes = [list_ref[i * DEPTH + k] for k in range(DEPTH)]
            tiles, states = [], []
            for code in codes:
                first = pl.multiple_of((jnp.right_shift(code, 5) & 31) * block_rows, block_rows)
                tiles.append(tiles_ref[code & 31])
                states.append(states_ref[pl.ds(first, block_rows), :])
            product = dot(jnp.concatenate(tiles, axis=1), jnp.concatenate(states, axis=0))
            target = jnp.right_shift(codes[0], 10)
            chunk = jnp.right_shift(target, 1) * 2
            for g in range(16):
                q, zl, c = g // 4, (g // 2) % 2, g % 2
                at = pl.ds(pl.multiple_of((target & 1) * 32 + q * 8, 8), 8)
                by_core[c][chunk + zl, at, :] += product[g * 8 : g * 8 + 8]
            return carry

        lax.fori_loop(0, steps, step, 0, unroll=steps)

    @pl.when(core_of(place_ref) == 0)
    def _():
        run((keep_ref, send_ref))

    @pl.when(core_of(place_ref) == 1)
    def _():
        run((send_ref, keep_ref))


def term(place, ids, targets, live, states, tiles):
    slots, _, blocks = ids.shape
    states_dev, members = states.shape
    steps = (slots * blocks + NLB * (DEPTH - 1)) // DEPTH
    half = jax.ShapeDtypeStruct((8, 64, members), F32)
    return pl.pallas_call(
        term_kernel,
        out_shape=(half, half),
        in_specs=[SMEM] + [HBM] * 5,
        out_specs=(VMEM, VMEM),
        scratch_shapes=[
            pltpu.SMEM(ids.shape, jnp.int32),
            pltpu.SMEM(ids.shape, jnp.int32),
            pltpu.SMEM(live.shape, jnp.int32),
            pltpu.VMEM((states_dev + tiles.shape[2], members), BF16),
            pltpu.VMEM(tiles.shape, BF16),
            pltpu.VMEM(ids.shape, jnp.int32),
            pltpu.SMEM((NLB,), jnp.int32),
            pltpu.SMEM((steps * DEPTH,), jnp.int32),
            pltpu.SemaphoreType.DMA((6,)),
        ],
        compiler_params=WHOLE,
        name="term",
    )(place, ids, targets, live, states, tiles)


def as_column(ref):
    count = ref.shape[1]
    at = lambda dim: lax.broadcasted_iota(jnp.int32, (count, count), dim)
    return jnp.sum(jnp.where(at(0) == at(1), ref[...], 0.0), axis=1, keepdims=True)


def copy_kernel(a_ref, out_ref):
    out_ref[...] = a_ref[...]


def add_kernel(a_ref, b_ref, out_ref):
    out_ref[...] = a_ref[...] + b_ref[...]


def rows_kernel(place_ref, parts_ref, counts_ref, var_ref, keep_ref, send_ref):
    total = jnp.sum(parts_ref[...], axis=0)
    rows, members = total.shape
    by_pair = total.reshape(rows // 16, 2, 8, members)
    first, second = (by_pair[:, p].reshape(rows // 2, members) for p in range(2))
    mine = pair_of(place_ref) == 0
    lane = lax.broadcasted_iota(jnp.int32, (8, 128), 1)
    counts, variance = as_column(counts_ref), as_column(var_ref)
    tail = jnp.where(lane == 0, counts, jnp.where(lane == 1, variance, 0.0))
    for ref, at, below in ((keep_ref, mine, tail), (send_ref, jnp.logical_not(mine), jnp.zeros_like(tail))):
        chosen = jnp.where(at, first, second)
        ref[0 : rows // 2, :] = chosen[:, :128]
        ref[rows // 2 : rows, :] = chosen[:, 128:]
        ref[rows:, :] = below


def gram_kernel(place_ref, parts_ref, out_ref):
    rows = (parts_ref.shape[1] - 8) // 2
    quads = parts_ref.shape[0] // 4
    groups = [[(2 * k + p) * 2 + c for k in range(quads)] for c in range(2) for p in range(2)]

    def whole(first):
        return jnp.concatenate([sum(parts_ref[m, first : first + rows, :] for m in g) for g in groups], axis=0)

    left, right = whole(0), whole(rows)
    tails = jnp.concatenate([parts_ref[m, 2 * rows :, :] for g in groups for m in g], axis=0)
    counts, variance = tails[:, 0:1], tails[:, 1:2]
    mean = jnp.sum(left + right, axis=1, keepdims=True) * (1.0 / 256.0)
    left, right = left - mean, right - mean
    weights = 1.0 / variance
    weighted = weights * (counts - mean)
    mine = core_of(place_ref) == 0
    own = jnp.where(mine, left, right)
    half = jnp.where(mine, left[:, :64], left[:, 64:])
    out_ref[0:16] = dot3(halves(own.T), halves(own * weights)).reshape(16, 8, 128)
    out_ref[16:24] = dot3(halves(half.T), halves(right * weights)).reshape(8, 8, 128)
    forcing = [jnp.sum(part * weighted, axis=0, keepdims=True) for part in (left, right)]
    out_ref[24] = jnp.concatenate([*forcing, jnp.zeros((6, 128), F32)], axis=0)
    out_ref[25:] = jnp.zeros((out_ref.shape[0] - 25, 8, 128), F32)


def share_kernel(parts_ref, out_ref):
    total = jnp.sum(parts_ref[...], axis=0)
    out_ref[...] = jnp.broadcast_to(total[None], out_ref.shape)


def update_kernel(place_ref, live_ref, pieces_ref, states_hbm, out_ref, states_ref, sem):
    own_rows, members = states_ref.shape
    own = pl.ds(pl.multiple_of(link_of(place_ref) * own_rows, own_rows), own_rows)
    copy = pltpu.make_async_copy(states_hbm.at[own], states_ref, sem)
    copy.start()
    by_core = pieces_ref[...].reshape(pieces_ref.shape[0] // 2, 2, 8, 128)
    first = by_core[0:16, 0].reshape(128, 128)
    last = by_core[0:16, 1].reshape(128, 128)
    across = jnp.concatenate([by_core[16:24, c].reshape(64, 128) for c in range(2)], axis=0)
    gram = jnp.concatenate(
        [jnp.concatenate([first, across], axis=1), jnp.concatenate([across.T, last], axis=1)], axis=0
    )
    forcing = jnp.concatenate([by_core[24, 0, 0:1], by_core[24, 0, 1:2]], axis=1)
    at = lambda dim: lax.broadcasted_iota(jnp.int32, (members, members), dim)
    diagonal = at(0) == at(1)
    identity = jnp.where(diagonal, 1.0, 0.0).astype(F32)
    forcing = jnp.sum(jnp.where(diagonal, forcing, 0.0), axis=1, keepdims=True)
    system = identity + gram * (1.0 / (members - 1.0))
    bound = jnp.max(jnp.sum(jnp.abs(system), axis=0, keepdims=True), axis=1, keepdims=True)
    root = system * (1.0 / bound)
    inverse = identity
    for sweep in range(NS_ITERS):
        if sweep == 0:
            middle = 1.5 * identity - 0.5 * root
            inverse = middle
        else:
            middle = 1.5 * identity - 0.5 * dot3(halves(inverse), halves(root))
        middle_halves = halves(middle)
        if sweep > 0:
            inverse = dot3(middle_halves, halves(inverse))
        if sweep < NS_ITERS - 1:
            root = dot3(halves(root), middle_halves)
    inner = jnp.sum(inverse * forcing, axis=0, keepdims=True)
    mean_weights = jnp.sum(inverse * inner, axis=1, keepdims=True) * (1.0 / (bound * (members - 1.0)))
    transform = inverse * lax.rsqrt(bound) + mean_weights
    transform += (1.0 - jnp.sum(transform, axis=0, keepdims=True)) * (1.0 / members)
    high, low = halves(transform)
    copy.wait()
    own_blocks = own_rows // 128
    position = lax.broadcasted_iota(jnp.int32, (128, members), 0)
    for k in range(own_blocks):
        rows = slice(k * 128, k * 128 + 128)
        states = states_ref[rows, :]
        updated = dot(states, high) + dot(states, low)
        live = live_ref[link_of(place_ref) * own_blocks + k]
        out_ref[rows, :] = jnp.where(position < live, updated, states.astype(F32)).astype(BF16)


def all_to_all(x, axes):
    return lax.all_to_all(x, axes, split_axis=0, concat_axis=0, tiled=True)


def local(kernel, shape, operands, scalars=0):
    return pl.pallas_call(
        kernel,
        out_shape=jax.ShapeDtypeStruct(shape, F32),
        in_specs=[SMEM] * scalars + [VMEM] * operands,
        out_specs=VMEM,
        compiler_params=PARAMS,
        name=kernel.__name__,
    )


def per_device(background, live_counts, patterns, pattern_ids, link_targets, counts_obs, obs_var):
    states_dev, members = background.shape
    place = lax.axis_index(("zp", "zl", "c", "x")).astype(jnp.int32).reshape(1)
    ids, targets = (jnp.transpose(a, (2, 0, 1)) for a in (pattern_ids, link_targets))
    keep, send = term(place, ids, targets, live_counts, background, patterns[0])
    received = lax.ppermute(send, "c", [(0, 1), (1, 0)])
    of_chip = local(add_kernel, keep.shape, 2)(local(copy_kernel, keep.shape, 1)(keep), received)
    parts = all_to_all(of_chip, ("y", "zl"))
    own, other = pl.pallas_call(
        rows_kernel,
        out_shape=(jax.ShapeDtypeStruct((72, 128), F32),) * 2,
        in_specs=[SMEM, VMEM, VMEM, VMEM],
        out_specs=(VMEM, VMEM),
        compiler_params=PARAMS,
        name="rows",
    )(place, parts, counts_obs, obs_var)
    own += lax.ppermute(other, "zp", [(0, 1), (1, 0)])
    column = lax.all_gather(own, ("zq", "zp", "c"))
    gram = local(gram_kernel, (32, 8, 128), 1, 1)(place, column)
    shared = local(share_kernel, (64, 8, 128), 1)(all_to_all(gram, ("x", "y", "zl")))
    pieces = all_to_all(shared, SLAB)
    own_rows = states_dev // lax.axis_size("x")
    return pl.pallas_call(
        update_kernel,
        out_shape=jax.ShapeDtypeStruct((own_rows, members), BF16),
        in_specs=[SMEM, SMEM, VMEM, HBM],
        out_specs=VMEM,
        scratch_shapes=[pltpu.VMEM((own_rows, members), BF16), pltpu.SemaphoreType.DMA],
        compiler_params=PARAMS,
        name="update",
    )(place, live_counts, pieces, background)


def solution(mesh):
    torus = Mesh(mesh.devices.reshape(4, 4, 2, 2, 2, 4), ("y", "zq", "zp", "zl", "c", "x"))
    return jax.shard_map(
        per_device,
        mesh=torus,
        in_specs=(
            P(ORIG, None),
            P(ORIG),
            P("x", ORIG, None, None),
            P("x", ORIG, None),
            P("x", ORIG, None),
            P("x", ORIG),
            P("x", ORIG),
        ),
        out_specs=P((*ORIG, "x"), None),
        check_vma=False,
    )
```

```python
import jax
import jax.numpy as jnp
from jax import lax
from jax.experimental import pallas as pl
from jax.experimental.pallas import tpu as pltpu
from jax.sharding import Mesh
from jax.sharding import PartitionSpec as P

NLB = 8
NS_ITERS = 4
F32 = jnp.float32
BF16 = jnp.bfloat16
ORIG = ("y", "zq", "zp", "zl", "c")
SLAB = ("x", "y", "zl", "c")
VMEM = pl.BlockSpec(memory_space=pltpu.VMEM)
SMEM = pl.BlockSpec(memory_space=pltpu.SMEM)
HBM = pl.BlockSpec(memory_space=pltpu.HBM)
DEPTH = 8
WHOLE = pltpu.CompilerParams(vmem_limit_bytes=58 * 2**20)
PARAMS = pltpu.CompilerParams(vmem_limit_bytes=40 * 2**20)


def halves(a):
    high = a.astype(BF16)
    return high, (a - high.astype(F32)).astype(BF16)


def dot(a, b):
    return jnp.dot(a, b, preferred_element_type=F32)


def dot3(a, b):
    (ah, al), (bh, bl) = a, b
    return dot(ah, bh) + (dot(ah, bl) + dot(al, bh))


def link_of(place_ref):
    return place_ref[0] & 3


def core_of(place_ref):
    return jnp.right_shift(place_ref[0], 2) & 1


def pair_of(place_ref):
    return jnp.right_shift(place_ref[0], 4) & 1


def term_kernel(
    place_ref, ids_hbm, targets_hbm, live_hbm, states_hbm, tiles_hbm, keep_ref, send_ref,
    ids_ref, targets_ref, live_ref, states_ref, tiles_ref, order_ref, list_ref, sems,
):
    slots, _, blocks = ids_ref.shape
    stored, link_rows, block_rows = tiles_ref.shape
    states_dev, members = states_hbm.shape
    entries = slots * blocks
    steps = (entries + NLB * (DEPTH - 1)) // DEPTH
    empty = float(blocks * stored)
    copies = [
        pltpu.make_async_copy(there, here, sems.at[i])
        for i, (there, here) in enumerate(
            (
                (ids_hbm, ids_ref),
                (targets_hbm, targets_ref),
                (live_hbm, live_ref),
                (states_hbm, states_ref.at[pl.ds(0, states_dev)]),
                (tiles_hbm, tiles_ref),
            )
        )
    ]
    for copy in copies:
        copy.start()
    keep_ref[...] = jnp.zeros_like(keep_ref)
    send_ref[...] = jnp.zeros_like(send_ref)
    states_ref[states_dev:, :] = jnp.zeros((block_rows, members), BF16)
    iota = lambda shape, dim: lax.broadcasted_iota(jnp.int32, shape, dim)
    square = (entries, entries)
    diagonal = iota(square, 0) == iota(square, 1)
    before = jnp.where(iota(square, 0) < iota(square, 1), 1.0, 0.0).astype(BF16)
    column = lambda row: jnp.sum(jnp.where(diagonal, row, 0.0), axis=1, keepdims=True)
    row = lambda a: jnp.concatenate([a[t] for t in range(slots)], axis=1).astype(F32)
    copies[0].wait()
    copies[1].wait()
    target = row(targets_ref[...])
    code = target * 1024.0 + row(iota(ids_ref.shape, 2) * stored + ids_ref[...])
    hits = jnp.where(iota((NLB, entries), 0).astype(F32) == target, 1.0, 0.0)
    rank = dot(hits.astype(BF16), before)
    needed = jnp.floor((jnp.sum(hits, axis=1, keepdims=True) + (DEPTH - 1)) * (1.0 / DEPTH)) * DEPTH
    starts = [jnp.zeros((1, 1), F32)]
    for j in range(NLB - 1):
        starts.append(starts[j] + needed[j : j + 1])
    places = jnp.sum(hits * (rank + jnp.concatenate(starts, axis=0)), axis=0, keepdims=True)
    put = column(places) == iota((entries, order_ref.shape[1]), 1).astype(F32)
    order = empty + jnp.sum(jnp.where(put, column(code) - empty, 0.0), axis=0, keepdims=True)
    order_ref[...] = order.astype(jnp.int32)
    ordered = pltpu.make_async_copy(order_ref, list_ref, sems.at[5])
    ordered.start()

    copies[2].wait()
    copies[3].wait()
    position = lax.broadcasted_iota(jnp.int32, (block_rows, members), 0)
    for b in range(blocks):
        rows = slice(b * block_rows, (b + 1) * block_rows)
        living = (position < live_ref[b]).astype(F32).astype(BF16)
        states_ref[rows, :] = states_ref[rows, :] * living
    copies[4].wait()
    ordered.wait()

    def run(by_core):
        def step(i, carry):
            codes = [list_ref[0, i * DEPTH + k] for k in range(DEPTH)]
            tiles, states = [], []
            for code in codes:
                first = pl.multiple_of((jnp.right_shift(code, 5) & 31) * block_rows, block_rows)
                tiles.append(tiles_ref[code & 31])
                states.append(states_ref[pl.ds(first, block_rows), :])
            product = dot(jnp.concatenate(tiles, axis=1), jnp.concatenate(states, axis=0))
            target = jnp.right_shift(codes[0], 10)
            chunk = jnp.right_shift(target, 1) * 2
            for g in range(16):
                q, zl, c = g // 4, (g // 2) % 2, g % 2
                at = pl.ds(pl.multiple_of((target & 1) * 32 + q * 8, 8), 8)
                by_core[c][chunk + zl, at, :] += product[g * 8 : g * 8 + 8]
            return carry

        lax.fori_loop(0, steps, step, 0, unroll=steps)

    @pl.when(core_of(place_ref) == 0)
    def _():
        run((keep_ref, send_ref))

    @pl.when(core_of(place_ref) == 1)
    def _():
        run((send_ref, keep_ref))


def term(place, ids, targets, live, states, tiles):
    slots, _, blocks = ids.shape
    states_dev, members = states.shape
    places = -(-(slots * blocks + NLB * (DEPTH - 1)) // 128) * 128
    half = jax.ShapeDtypeStruct((8, 64, members), F32)
    return pl.pallas_call(
        term_kernel,
        out_shape=(half, half),
        in_specs=[SMEM] + [HBM] * 5,
        out_specs=(VMEM, VMEM),
        scratch_shapes=[
            pltpu.VMEM(ids.shape, jnp.int32),
            pltpu.VMEM(ids.shape, jnp.int32),
            pltpu.SMEM(live.shape, jnp.int32),
            pltpu.VMEM((states_dev + tiles.shape[2], members), BF16),
            pltpu.VMEM(tiles.shape, BF16),
            pltpu.VMEM((1, places), jnp.int32),
            pltpu.SMEM((1, places), jnp.int32),
            pltpu.SemaphoreType.DMA((6,)),
        ],
        compiler_params=WHOLE,
        name="term",
    )(place, ids, targets, live, states, tiles)


def as_column(ref):
    count = ref.shape[1]
    at = lambda dim: lax.broadcasted_iota(jnp.int32, (count, count), dim)
    return jnp.sum(jnp.where(at(0) == at(1), ref[...], 0.0), axis=1, keepdims=True)


def copy_kernel(a_ref, out_ref):
    out_ref[...] = a_ref[...]


def add_kernel(a_ref, b_ref, out_ref):
    out_ref[...] = a_ref[...] + b_ref[...]


def rows_kernel(place_ref, parts_ref, counts_ref, var_ref, keep_ref, send_ref):
    total = jnp.sum(parts_ref[...], axis=0)
    rows, members = total.shape
    by_pair = total.reshape(rows // 16, 2, 8, members)
    first, second = (by_pair[:, p].reshape(rows // 2, members) for p in range(2))
    mine = pair_of(place_ref) == 0
    lane = lax.broadcasted_iota(jnp.int32, (8, 128), 1)
    counts, variance = as_column(counts_ref), as_column(var_ref)
    tail = jnp.where(lane == 0, counts, jnp.where(lane == 1, variance, 0.0))
    for ref, at, below in ((keep_ref, mine, tail), (send_ref, jnp.logical_not(mine), jnp.zeros_like(tail))):
        chosen = jnp.where(at, first, second)
        ref[0 : rows // 2, :] = chosen[:, :128]
        ref[rows // 2 : rows, :] = chosen[:, 128:]
        ref[rows:, :] = below


def gram_kernel(place_ref, parts_ref, out_ref):
    rows = (parts_ref.shape[1] - 8) // 2
    quads = parts_ref.shape[0] // 4
    groups = [[(2 * k + p) * 2 + c for k in range(quads)] for c in range(2) for p in range(2)]

    def whole(first):
        return jnp.concatenate([sum(parts_ref[m, first : first + rows, :] for m in g) for g in groups], axis=0)

    left, right = whole(0), whole(rows)
    tails = jnp.concatenate([parts_ref[m, 2 * rows :, :] for g in groups for m in g], axis=0)
    counts, variance = tails[:, 0:1], tails[:, 1:2]
    mean = jnp.sum(left + right, axis=1, keepdims=True) * (1.0 / 256.0)
    left, right = left - mean, right - mean
    weights = 1.0 / variance
    weighted = weights * (counts - mean)
    mine = core_of(place_ref) == 0
    own = jnp.where(mine, left, right)
    half = jnp.where(mine, left[:, :64], left[:, 64:])
    out_ref[0:16] = dot3(halves(own.T), halves(own * weights)).reshape(16, 8, 128)
    out_ref[16:24] = dot3(halves(half.T), halves(right * weights)).reshape(8, 8, 128)
    forcing = [jnp.sum(part * weighted, axis=0, keepdims=True) for part in (left, right)]
    out_ref[24] = jnp.concatenate([*forcing, jnp.zeros((6, 128), F32)], axis=0)
    out_ref[25:] = jnp.zeros((out_ref.shape[0] - 25, 8, 128), F32)


def share_kernel(parts_ref, out_ref):
    total = jnp.sum(parts_ref[...], axis=0)
    out_ref[...] = jnp.broadcast_to(total[None], out_ref.shape)


def update_kernel(place_ref, live_hbm, pieces_ref, states_hbm, out_ref, states_ref, live_ref, sems):
    own_rows, members = states_ref.shape
    own = pl.ds(pl.multiple_of(link_of(place_ref) * own_rows, own_rows), own_rows)
    copies = (
        pltpu.make_async_copy(states_hbm.at[own], states_ref, sems.at[0]),
        pltpu.make_async_copy(live_hbm, live_ref, sems.at[1]),
    )
    for copy in copies:
        copy.start()
    by_core = pieces_ref[...].reshape(pieces_ref.shape[0] // 2, 2, 8, 128)
    first = by_core[0:16, 0].reshape(128, 128)
    last = by_core[0:16, 1].reshape(128, 128)
    across = jnp.concatenate([by_core[16:24, c].reshape(64, 128) for c in range(2)], axis=0)
    gram = jnp.concatenate(
        [jnp.concatenate([first, across], axis=1), jnp.concatenate([across.T, last], axis=1)], axis=0
    )
    forcing = jnp.concatenate([by_core[24, 0, 0:1], by_core[24, 0, 1:2]], axis=1)
    at = lambda dim: lax.broadcasted_iota(jnp.int32, (members, members), dim)
    diagonal = at(0) == at(1)
    identity = jnp.where(diagonal, 1.0, 0.0).astype(F32)
    forcing = jnp.sum(jnp.where(diagonal, forcing, 0.0), axis=1, keepdims=True)
    system = identity + gram * (1.0 / (members - 1.0))
    bound = jnp.max(jnp.sum(jnp.abs(system), axis=0, keepdims=True), axis=1, keepdims=True)
    root = system * (1.0 / bound)
    inverse = identity
    for sweep in range(NS_ITERS):
        if sweep == 0:
            middle = 1.5 * identity - 0.5 * root
            inverse = middle
        else:
            middle = 1.5 * identity - 0.5 * dot3(halves(inverse), halves(root))
        middle_halves = halves(middle)
        if sweep > 0:
            inverse = dot3(middle_halves, halves(inverse))
        if sweep < NS_ITERS - 1:
            root = dot3(halves(root), middle_halves)
    inner = jnp.sum(inverse * forcing, axis=0, keepdims=True)
    mean_weights = jnp.sum(inverse * inner, axis=1, keepdims=True) * (1.0 / (bound * (members - 1.0)))
    transform = inverse * lax.rsqrt(bound) + mean_weights
    transform += (1.0 - jnp.sum(transform, axis=0, keepdims=True)) * (1.0 / members)
    high, low = halves(transform)
    for copy in copies:
        copy.wait()
    own_blocks = own_rows // 128
    position = lax.broadcasted_iota(jnp.int32, (128, members), 0)
    for k in range(own_blocks):
        rows = slice(k * 128, k * 128 + 128)
        states = states_ref[rows, :]
        updated = dot(states, high) + dot(states, low)
        live = live_ref[link_of(place_ref) * own_blocks + k]
        out_ref[rows, :] = jnp.where(position < live, updated, states.astype(F32)).astype(BF16)


def all_to_all(x, axes):
    return lax.all_to_all(x, axes, split_axis=0, concat_axis=0, tiled=True)


def local(kernel, shape, operands, scalars=0):
    return pl.pallas_call(
        kernel,
        out_shape=jax.ShapeDtypeStruct(shape, F32),
        in_specs=[SMEM] * scalars + [VMEM] * operands,
        out_specs=VMEM,
        compiler_params=PARAMS,
        name=kernel.__name__,
    )


def per_device(background, live_counts, patterns, pattern_ids, link_targets, counts_obs, obs_var):
    states_dev, members = background.shape
    place = lax.axis_index(("zp", "zl", "c", "x")).astype(jnp.int32).reshape(1)
    ids, targets = (jnp.transpose(a, (2, 0, 1)) for a in (pattern_ids, link_targets))
    keep, send = term(place, ids, targets, live_counts, background, patterns[0])
    received = lax.ppermute(send, "c", [(0, 1), (1, 0)])
    of_chip = local(add_kernel, keep.shape, 2)(local(copy_kernel, keep.shape, 1)(keep), received)
    parts = all_to_all(of_chip, ("y", "zl"))
    own, other = pl.pallas_call(
        rows_kernel,
        out_shape=(jax.ShapeDtypeStruct((72, 128), F32),) * 2,
        in_specs=[SMEM, VMEM, VMEM, VMEM],
        out_specs=(VMEM, VMEM),
        compiler_params=PARAMS,
        name="rows",
    )(place, parts, counts_obs, obs_var)
    own += lax.ppermute(other, "zp", [(0, 1), (1, 0)])
    column = lax.all_gather(own, ("zq", "zp", "c"))
    gram = local(gram_kernel, (32, 8, 128), 1, 1)(place, column)
    shared = local(share_kernel, (64, 8, 128), 1)(all_to_all(gram, ("x", "y", "zl")))
    pieces = all_to_all(shared, SLAB)
    own_rows = states_dev // lax.axis_size("x")
    return pl.pallas_call(
        update_kernel,
        out_shape=jax.ShapeDtypeStruct((own_rows, members), BF16),
        in_specs=[SMEM, HBM, VMEM, HBM],
        out_specs=VMEM,
        scratch_shapes=[
            pltpu.VMEM((own_rows, members), BF16),
            pltpu.SMEM(live_counts.shape, jnp.int32),
            pltpu.SemaphoreType.DMA((2,)),
        ],
        compiler_params=PARAMS,
        name="update",
    )(place, live_counts, pieces, background)


def solution(mesh):
    torus = Mesh(mesh.devices.reshape(4, 4, 2, 2, 2, 4), ("y", "zq", "zp", "zl", "c", "x"))
    return jax.shard_map(
        per_device,
        mesh=torus,
        in_specs=(
            P(ORIG, None),
            P(ORIG),
            P("x", ORIG, None, None),
            P("x", ORIG, None),
            P("x", ORIG, None),
            P("x", ORIG),
            P("x", ORIG),
        ),
        out_specs=P((*ORIG, "x"), None),
        check_vma=False,
    )
```

```python
import jax
import jax.numpy as jnp
from jax import lax
from jax.experimental import pallas as pl
from jax.experimental.pallas import tpu as pltpu
from jax.sharding import Mesh
from jax.sharding import PartitionSpec as P

NLB = 8
NS_ITERS = 4
F32 = jnp.float32
BF16 = jnp.bfloat16
ORIG = ("y", "zq", "zp", "zl", "c")
SLAB = ("x", "y", "zl", "c")
VMEM = pl.BlockSpec(memory_space=pltpu.VMEM)
SMEM = pl.BlockSpec(memory_space=pltpu.SMEM)
HBM = pl.BlockSpec(memory_space=pltpu.HBM)
DEPTH = 8
WHOLE = pltpu.CompilerParams(vmem_limit_bytes=58 * 2**20)
PARAMS = pltpu.CompilerParams(vmem_limit_bytes=40 * 2**20)


def halves(a):
    high = a.astype(BF16)
    return high, (a - high.astype(F32)).astype(BF16)


def dot(a, b):
    return jnp.dot(a, b, preferred_element_type=F32)


def dot3(a, b):
    (ah, al), (bh, bl) = a, b
    return dot(ah, bh) + (dot(ah, bl) + dot(al, bh))


def link_of(place_ref):
    return place_ref[0] & 3


def core_of(place_ref):
    return jnp.right_shift(place_ref[0], 2) & 1


def side_of(place_ref):
    return jnp.right_shift(place_ref[0], 3) & 1


def pair_of(place_ref):
    return jnp.right_shift(place_ref[0], 4) & 1


def term_kernel(
    place_ref, ids_hbm, targets_hbm, live_hbm, states_hbm, tiles_hbm, keep_ref, send_ref,
    ids_ref, targets_ref, live_ref, states_ref, tiles_ref, order_ref, list_ref, sems,
):
    slots, _, blocks = ids_ref.shape
    stored, link_rows, block_rows = tiles_ref.shape
    states_dev, members = states_hbm.shape
    entries = slots * blocks
    steps = (entries + NLB * (DEPTH - 1)) // DEPTH
    empty = float(blocks * stored)
    copies = [
        pltpu.make_async_copy(there, here, sems.at[i])
        for i, (there, here) in enumerate(
            (
                (ids_hbm, ids_ref),
                (targets_hbm, targets_ref),
                (live_hbm, live_ref),
                (states_hbm, states_ref.at[pl.ds(0, states_dev)]),
                (tiles_hbm, tiles_ref),
            )
        )
    ]
    for copy in copies:
        copy.start()
    keep_ref[...] = jnp.zeros_like(keep_ref)
    send_ref[...] = jnp.zeros_like(send_ref)
    states_ref[states_dev:, :] = jnp.zeros((block_rows, members), BF16)
    iota = lambda shape, dim: lax.broadcasted_iota(jnp.int32, shape, dim)
    square = (entries, entries)
    diagonal = iota(square, 0) == iota(square, 1)
    before = jnp.where(iota(square, 0) < iota(square, 1), 1.0, 0.0).astype(BF16)
    column = lambda row: jnp.sum(jnp.where(diagonal, row, 0.0), axis=1, keepdims=True)
    row = lambda a: jnp.concatenate([a[t] for t in range(slots)], axis=1).astype(F32)
    copies[0].wait()
    copies[1].wait()
    target = row(targets_ref[...])
    code = target * 1024.0 + row(iota(ids_ref.shape, 2) * stored + ids_ref[...])
    hits = jnp.where(iota((NLB, entries), 0).astype(F32) == target, 1.0, 0.0)
    rank = dot(hits.astype(BF16), before)
    needed = jnp.floor((jnp.sum(hits, axis=1, keepdims=True) + (DEPTH - 1)) * (1.0 / DEPTH)) * DEPTH
    starts = [jnp.zeros((1, 1), F32)]
    for j in range(NLB - 1):
        starts.append(starts[j] + needed[j : j + 1])
    places = jnp.sum(hits * (rank + jnp.concatenate(starts, axis=0)), axis=0, keepdims=True)
    put = column(places) == iota((entries, order_ref.shape[1]), 1).astype(F32)
    order = empty + jnp.sum(jnp.where(put, column(code) - empty, 0.0), axis=0, keepdims=True)
    order_ref[...] = order.astype(jnp.int32)
    ordered = pltpu.make_async_copy(order_ref, list_ref, sems.at[5])
    ordered.start()

    copies[2].wait()
    copies[3].wait()
    position = lax.broadcasted_iota(jnp.int32, (block_rows, members), 0)
    for b in range(blocks):
        rows = slice(b * block_rows, (b + 1) * block_rows)
        living = (position < live_ref[b]).astype(F32).astype(BF16)
        states_ref[rows, :] = states_ref[rows, :] * living
    copies[4].wait()
    ordered.wait()

    pair = pair_of(place_ref)

    def run(by_core):
        def step(i, carry):
            codes = [list_ref[0, i * DEPTH + k] for k in range(DEPTH)]
            tiles, states = [], []
            for code in codes:
                first = pl.multiple_of((jnp.right_shift(code, 5) & 31) * block_rows, block_rows)
                tiles.append(tiles_ref[code & 31])
                states.append(states_ref[pl.ds(first, block_rows), :])
            product = dot(jnp.concatenate(tiles, axis=1), jnp.concatenate(states, axis=0))
            target = jnp.right_shift(codes[0], 10)
            chunk = jnp.right_shift(target, 1) * 2
            for g in range(16):
                h, p, l, c = g // 8, (g // 4) % 2, (g // 2) % 2, g % 2
                at = pl.ds(pl.multiple_of((target & 1) * 32 + h * 16 + l * 8, 8), 8)
                by_core[c][chunk + (p ^ pair), at, :] += product[g * 8 : g * 8 + 8]
            return carry

        lax.fori_loop(0, steps, step, 0, unroll=steps)

    @pl.when(core_of(place_ref) == 0)
    def _():
        run((keep_ref, send_ref))

    @pl.when(core_of(place_ref) == 1)
    def _():
        run((send_ref, keep_ref))


def term(place, ids, targets, live, states, tiles):
    slots, _, blocks = ids.shape
    states_dev, members = states.shape
    places = -(-(slots * blocks + NLB * (DEPTH - 1)) // 128) * 128
    half = jax.ShapeDtypeStruct((8, 64, members), F32)
    return pl.pallas_call(
        term_kernel,
        out_shape=(half, half),
        in_specs=[SMEM] + [HBM] * 5,
        out_specs=(VMEM, VMEM),
        scratch_shapes=[
            pltpu.VMEM(ids.shape, jnp.int32),
            pltpu.VMEM(ids.shape, jnp.int32),
            pltpu.SMEM(live.shape, jnp.int32),
            pltpu.VMEM((states_dev + tiles.shape[2], members), BF16),
            pltpu.VMEM(tiles.shape, BF16),
            pltpu.VMEM((1, places), jnp.int32),
            pltpu.SMEM((1, places), jnp.int32),
            pltpu.SemaphoreType.DMA((6,)),
        ],
        compiler_params=WHOLE,
        name="term",
    )(place, ids, targets, live, states, tiles)


def as_column(ref):
    count = ref.shape[1]
    at = lambda dim: lax.broadcasted_iota(jnp.int32, (count, count), dim)
    return jnp.sum(jnp.where(at(0) == at(1), ref[...], 0.0), axis=1, keepdims=True)


def copy_kernel(a_ref, out_ref):
    out_ref[...] = a_ref[...]


def add_kernel(a_ref, b_ref, out_ref):
    out_ref[...] = a_ref[...] + b_ref[...]


def rows_kernel(place_ref, parts_ref, counts_ref, var_ref, keep_ref, send_ref):
    total = jnp.sum(parts_ref[...], axis=0)
    rows, members = total.shape
    by_pair = total.reshape(rows // 16, 2, 8, members)
    first, second = (by_pair[:, p].reshape(rows // 2, members) for p in range(2))
    mine = side_of(place_ref) == 0
    lane = lax.broadcasted_iota(jnp.int32, (8, 128), 1)
    counts, variance = as_column(counts_ref), as_column(var_ref)
    tail = jnp.where(lane == 0, counts, jnp.where(lane == 1, variance, 0.0))
    for ref, at, below in ((keep_ref, mine, tail), (send_ref, jnp.logical_not(mine), jnp.zeros_like(tail))):
        chosen = jnp.where(at, first, second)
        ref[0 : rows // 2, :] = chosen[:, :128]
        ref[rows // 2 : rows, :] = chosen[:, 128:]
        ref[rows:, :] = below


def gram_kernel(place_ref, parts_ref, out_ref):
    rows = (parts_ref.shape[1] - 8) // 2
    quads = parts_ref.shape[0] // 4
    groups = [[(2 * k + p) * 2 + c for k in range(quads)] for c in range(2) for p in range(2)]

    def whole(first):
        return jnp.concatenate([sum(parts_ref[m, first : first + rows, :] for m in g) for g in groups], axis=0)

    left, right = whole(0), whole(rows)
    tail = lambda g: jnp.concatenate([parts_ref[m, 2 * rows :, :] for m in g], axis=0)
    straight = side_of(place_ref) == 0
    tails = jnp.concatenate(
        [jnp.where(straight, tail(groups[k]), tail(groups[k ^ 1])) for k in range(len(groups))], axis=0
    )
    counts, variance = tails[:, 0:1], tails[:, 1:2]
    mean = jnp.sum(left + right, axis=1, keepdims=True) * (1.0 / 256.0)
    left, right = left - mean, right - mean
    weights = 1.0 / variance
    weighted = weights * (counts - mean)
    mine = core_of(place_ref) == 0
    own = jnp.where(mine, left, right)
    half = jnp.where(mine, left[:, :64], left[:, 64:])
    out_ref[0:16] = dot3(halves(own.T), halves(own * weights)).reshape(16, 8, 128)
    out_ref[16:24] = dot3(halves(half.T), halves(right * weights)).reshape(8, 8, 128)
    forcing = [jnp.sum(part * weighted, axis=0, keepdims=True) for part in (left, right)]
    out_ref[24] = jnp.concatenate([*forcing, jnp.zeros((6, 128), F32)], axis=0)
    out_ref[25:] = jnp.zeros((out_ref.shape[0] - 25, 8, 128), F32)


def share_kernel(parts_ref, out_ref):
    total = jnp.sum(parts_ref[...], axis=0)
    out_ref[...] = jnp.broadcast_to(total[None], out_ref.shape)


def update_kernel(place_ref, live_hbm, pieces_ref, states_hbm, out_ref, states_ref, live_ref, sems):
    own_rows, members = states_ref.shape
    own = pl.ds(pl.multiple_of(link_of(place_ref) * own_rows, own_rows), own_rows)
    copies = (
        pltpu.make_async_copy(states_hbm.at[own], states_ref, sems.at[0]),
        pltpu.make_async_copy(live_hbm, live_ref, sems.at[1]),
    )
    for copy in copies:
        copy.start()
    by_core = pieces_ref[...].reshape(pieces_ref.shape[0] // 2, 2, 8, 128)
    first = by_core[0:16, 0].reshape(128, 128)
    last = by_core[0:16, 1].reshape(128, 128)
    across = jnp.concatenate([by_core[16:24, c].reshape(64, 128) for c in range(2)], axis=0)
    gram = jnp.concatenate(
        [jnp.concatenate([first, across], axis=1), jnp.concatenate([across.T, last], axis=1)], axis=0
    )
    forcing = jnp.concatenate([by_core[24, 0, 0:1], by_core[24, 0, 1:2]], axis=1)
    at = lambda dim: lax.broadcasted_iota(jnp.int32, (members, members), dim)
    diagonal = at(0) == at(1)
    identity = jnp.where(diagonal, 1.0, 0.0).astype(F32)
    forcing = jnp.sum(jnp.where(diagonal, forcing, 0.0), axis=1, keepdims=True)
    system = identity + gram * (1.0 / (members - 1.0))
    bound = jnp.max(jnp.sum(jnp.abs(system), axis=0, keepdims=True), axis=1, keepdims=True)
    root = system * (1.0 / bound)
    inverse = identity
    for sweep in range(NS_ITERS):
        if sweep == 0:
            middle = 1.5 * identity - 0.5 * root
            inverse = middle
        else:
            middle = 1.5 * identity - 0.5 * dot3(halves(inverse), halves(root))
        middle_halves = halves(middle)
        if sweep > 0:
            inverse = dot3(middle_halves, halves(inverse))
        if sweep < NS_ITERS - 1:
            root = dot3(halves(root), middle_halves)
    inner = jnp.sum(inverse * forcing, axis=0, keepdims=True)
    mean_weights = jnp.sum(inverse * inner, axis=1, keepdims=True) * (1.0 / (bound * (members - 1.0)))
    transform = inverse * lax.rsqrt(bound) + mean_weights
    transform += (1.0 - jnp.sum(transform, axis=0, keepdims=True)) * (1.0 / members)
    high, low = halves(transform)
    for copy in copies:
        copy.wait()
    own_blocks = own_rows // 128
    position = lax.broadcasted_iota(jnp.int32, (128, members), 0)
    for k in range(own_blocks):
        rows = slice(k * 128, k * 128 + 128)
        states = states_ref[rows, :]
        updated = dot(states, high) + dot(states, low)
        live = live_ref[link_of(place_ref) * own_blocks + k]
        out_ref[rows, :] = jnp.where(position < live, updated, states.astype(F32)).astype(BF16)


def all_to_all(x, axes):
    return lax.all_to_all(x, axes, split_axis=0, concat_axis=0, tiled=True)


def local(kernel, shape, operands, scalars=0):
    return pl.pallas_call(
        kernel,
        out_shape=jax.ShapeDtypeStruct(shape, F32),
        in_specs=[SMEM] * scalars + [VMEM] * operands,
        out_specs=VMEM,
        compiler_params=PARAMS,
        name=kernel.__name__,
    )


def per_device(background, live_counts, patterns, pattern_ids, link_targets, counts_obs, obs_var):
    states_dev, members = background.shape
    place = lax.axis_index(("zp", "zl", "c", "x")).astype(jnp.int32).reshape(1)
    ids, targets = (jnp.transpose(a, (2, 0, 1)) for a in (pattern_ids, link_targets))
    keep, send = term(place, ids, targets, live_counts, background, patterns[0])
    received = lax.ppermute(send, "c", [(0, 1), (1, 0)])
    of_chip = local(add_kernel, keep.shape, 2)(local(copy_kernel, keep.shape, 1)(keep), received)
    parts = all_to_all(of_chip, ("y", "zl"))
    own, other = pl.pallas_call(
        rows_kernel,
        out_shape=(jax.ShapeDtypeStruct((72, 128), F32),) * 2,
        in_specs=[SMEM, VMEM, VMEM, VMEM],
        out_specs=(VMEM, VMEM),
        compiler_params=PARAMS,
        name="rows",
    )(place, parts, counts_obs, obs_var)
    own += lax.ppermute(other, ("zq", "zp", "zl"), [(z, (z + (1 if z % 2 else -1)) % 16) for z in range(16)])
    column = lax.all_gather(own, ("zq", "zp", "c"))
    gram = local(gram_kernel, (32, 8, 128), 1, 1)(place, column)
    shared = local(share_kernel, (64, 8, 128), 1)(all_to_all(gram, ("x", "y", "zl")))
    pieces = all_to_all(shared, SLAB)
    own_rows = states_dev // lax.axis_size("x")
    return pl.pallas_call(
        update_kernel,
        out_shape=jax.ShapeDtypeStruct((own_rows, members), BF16),
        in_specs=[SMEM, HBM, VMEM, HBM],
        out_specs=VMEM,
        scratch_shapes=[
            pltpu.VMEM((own_rows, members), BF16),
            pltpu.SMEM(live_counts.shape, jnp.int32),
            pltpu.SemaphoreType.DMA((2,)),
        ],
        compiler_params=PARAMS,
        name="update",
    )(place, live_counts, pieces, background)


def solution(mesh):
    torus = Mesh(mesh.devices.reshape(4, 4, 2, 2, 2, 4), ("y", "zq", "zp", "zl", "c", "x"))
    return jax.shard_map(
        per_device,
        mesh=torus,
        in_specs=(
            P(ORIG, None),
            P(ORIG),
            P("x", ORIG, None, None),
            P("x", ORIG, None),
            P("x", ORIG, None),
            P("x", ORIG),
            P("x", ORIG),
        ),
        out_specs=P((*ORIG, "x"), None),
        check_vma=False,
    )
```

```python
import jax
import jax.numpy as jnp
from jax import lax
from jax.experimental import pallas as pl
from jax.experimental.pallas import tpu as pltpu
from jax.sharding import Mesh
from jax.sharding import PartitionSpec as P

NLB = 8
NS_ITERS = 4
F32 = jnp.float32
BF16 = jnp.bfloat16
ORIG = ("y", "zq", "zp", "zl", "c")
SLAB = ("x", "y", "zl", "c")
VMEM = pl.BlockSpec(memory_space=pltpu.VMEM)
SMEM = pl.BlockSpec(memory_space=pltpu.SMEM)
HBM = pl.BlockSpec(memory_space=pltpu.HBM)
DEPTH = 8
WHOLE = pltpu.CompilerParams(vmem_limit_bytes=58 * 2**20)
PARAMS = pltpu.CompilerParams(vmem_limit_bytes=40 * 2**20)


def halves(a):
    high = a.astype(BF16)
    return high, (a - high.astype(F32)).astype(BF16)


def dot(a, b):
    return jnp.dot(a, b, preferred_element_type=F32)


def dot3(a, b, dot=dot):
    (ah, al), (bh, bl) = a, b
    return dot(ah, bh) + (dot(ah, bl) + dot(al, bh))


def over_rows(a, b):
    return lax.dot_general(a, b, (((0,), (0,)), ((), ())), preferred_element_type=F32)


def link_of(place_ref):
    return place_ref[0] & 3


def core_of(place_ref):
    return jnp.right_shift(place_ref[0], 2) & 1


def side_of(place_ref):
    return jnp.right_shift(place_ref[0], 3) & 1


def pair_of(place_ref):
    return jnp.right_shift(place_ref[0], 4) & 1


def term_kernel(
    place_ref, ids_hbm, targets_hbm, live_hbm, states_hbm, tiles_hbm, keep_ref, send_ref,
    ids_ref, targets_ref, live_ref, states_ref, tiles_ref, order_ref, list_ref, sems,
):
    slots, _, blocks = ids_ref.shape
    stored, link_rows, block_rows = tiles_ref.shape
    states_dev, members = states_hbm.shape
    entries = slots * blocks
    steps = (entries + NLB * (DEPTH - 1)) // DEPTH
    empty = float(blocks * stored)
    copies = [
        pltpu.make_async_copy(there, here, sems.at[i])
        for i, (there, here) in enumerate(
            (
                (ids_hbm, ids_ref),
                (targets_hbm, targets_ref),
                (live_hbm, live_ref),
                (states_hbm, states_ref.at[pl.ds(0, states_dev)]),
                (tiles_hbm, tiles_ref),
            )
        )
    ]
    for copy in copies:
        copy.start()
    keep_ref[...] = jnp.zeros_like(keep_ref)
    send_ref[...] = jnp.zeros_like(send_ref)
    states_ref[states_dev:, :] = jnp.zeros((block_rows, members), BF16)
    iota = lambda shape, dim: lax.broadcasted_iota(jnp.int32, shape, dim)
    square = (entries, entries)
    diagonal = iota(square, 0) == iota(square, 1)
    before = jnp.where(iota(square, 0) < iota(square, 1), 1.0, 0.0).astype(BF16)
    column = lambda row: jnp.sum(jnp.where(diagonal, row, 0.0), axis=1, keepdims=True)
    row = lambda a: jnp.concatenate([a[t] for t in range(slots)], axis=1).astype(F32)
    copies[0].wait()
    copies[1].wait()
    target = row(targets_ref[...])
    code = target * 1024.0 + row(iota(ids_ref.shape, 2) * stored + ids_ref[...])
    hits = jnp.where(iota((NLB, entries), 0).astype(F32) == target, 1.0, 0.0)
    rank = dot(hits.astype(BF16), before)
    needed = jnp.floor((jnp.sum(hits, axis=1, keepdims=True) + (DEPTH - 1)) * (1.0 / DEPTH)) * DEPTH
    starts = [jnp.zeros((1, 1), F32)]
    for j in range(NLB - 1):
        starts.append(starts[j] + needed[j : j + 1])
    places = jnp.sum(hits * (rank + jnp.concatenate(starts, axis=0)), axis=0, keepdims=True)
    put = column(places) == iota((entries, order_ref.shape[1]), 1).astype(F32)
    order = empty + jnp.sum(jnp.where(put, column(code) - empty, 0.0), axis=0, keepdims=True)
    order_ref[...] = order.astype(jnp.int32)
    ordered = pltpu.make_async_copy(order_ref, list_ref, sems.at[5])
    ordered.start()

    copies[2].wait()
    copies[3].wait()
    position = lax.broadcasted_iota(jnp.int32, (block_rows, members), 0)
    for b in range(blocks):
        rows = slice(b * block_rows, (b + 1) * block_rows)
        living = (position < live_ref[b]).astype(F32).astype(BF16)
        states_ref[rows, :] = states_ref[rows, :] * living
    copies[4].wait()
    ordered.wait()

    pair = pair_of(place_ref)

    def run(by_core):
        def step(i, carry):
            codes = [list_ref[0, i * DEPTH + k] for k in range(DEPTH)]
            tiles, states = [], []
            for code in codes:
                first = pl.multiple_of((jnp.right_shift(code, 5) & 31) * block_rows, block_rows)
                tiles.append(tiles_ref[code & 31])
                states.append(states_ref[pl.ds(first, block_rows), :])
            product = dot(jnp.concatenate(tiles, axis=1), jnp.concatenate(states, axis=0))
            target = jnp.right_shift(codes[0], 10)
            chunk = jnp.right_shift(target, 1) * 2
            for g in range(16):
                h, p, l, c = g // 8, (g // 4) % 2, (g // 2) % 2, g % 2
                at = pl.ds(pl.multiple_of((target & 1) * 32 + h * 16 + l * 8, 8), 8)
                by_core[c][chunk + (p ^ pair), at, :] += product[g * 8 : g * 8 + 8]
            return carry

        lax.fori_loop(0, steps, step, 0, unroll=steps)

    @pl.when(core_of(place_ref) == 0)
    def _():
        run((keep_ref, send_ref))

    @pl.when(core_of(place_ref) == 1)
    def _():
        run((send_ref, keep_ref))


def term(place, ids, targets, live, states, tiles):
    slots, _, blocks = ids.shape
    states_dev, members = states.shape
    places = -(-(slots * blocks + NLB * (DEPTH - 1)) // 128) * 128
    half = jax.ShapeDtypeStruct((8, 64, members), F32)
    return pl.pallas_call(
        term_kernel,
        out_shape=(half, half),
        in_specs=[SMEM] + [HBM] * 5,
        out_specs=(VMEM, VMEM),
        scratch_shapes=[
            pltpu.VMEM(ids.shape, jnp.int32),
            pltpu.VMEM(ids.shape, jnp.int32),
            pltpu.SMEM(live.shape, jnp.int32),
            pltpu.VMEM((states_dev + tiles.shape[2], members), BF16),
            pltpu.VMEM(tiles.shape, BF16),
            pltpu.VMEM((1, places), jnp.int32),
            pltpu.SMEM((1, places), jnp.int32),
            pltpu.SemaphoreType.DMA((6,)),
        ],
        compiler_params=WHOLE,
        name="term",
    )(place, ids, targets, live, states, tiles)


def as_column(ref):
    count = ref.shape[1]
    at = lambda dim: lax.broadcasted_iota(jnp.int32, (count, count), dim)
    return jnp.sum(jnp.where(at(0) == at(1), ref[...], 0.0), axis=1, keepdims=True)


def copy_kernel(a_ref, out_ref):
    out_ref[...] = a_ref[...]


def add_kernel(a_ref, b_ref, out_ref):
    out_ref[...] = a_ref[...] + b_ref[...]


def rows_kernel(place_ref, parts_ref, counts_ref, var_ref, keep_ref, send_ref):
    total = jnp.sum(parts_ref[...], axis=0)
    rows, members = total.shape
    by_pair = total.reshape(rows // 16, 2, 8, members)
    first, second = (by_pair[:, p].reshape(rows // 2, members) for p in range(2))
    mine = side_of(place_ref) == 0
    lane = lax.broadcasted_iota(jnp.int32, (8, 128), 1)
    counts, variance = as_column(counts_ref), as_column(var_ref)
    tail = jnp.where(lane == 0, counts, jnp.where(lane == 1, variance, 0.0))
    for ref, at, below in ((keep_ref, mine, tail), (send_ref, jnp.logical_not(mine), jnp.zeros_like(tail))):
        chosen = jnp.where(at, first, second)
        ref[0 : rows // 2, :] = chosen[:, :128]
        ref[rows // 2 : rows, :] = chosen[:, 128:]
        ref[rows:, :] = below


def gram_kernel(place_ref, parts_ref, out_ref):
    rows = (parts_ref.shape[1] - 8) // 2
    quads = parts_ref.shape[0] // 4
    groups = [[(2 * k + p) * 2 + c for k in range(quads)] for c in range(2) for p in range(2)]

    def whole(first):
        return jnp.concatenate([sum(parts_ref[m, first : first + rows, :] for m in g) for g in groups], axis=0)

    left, right = whole(0), whole(rows)
    tail = lambda g: jnp.concatenate([parts_ref[m, 2 * rows :, :] for m in g], axis=0)
    straight = side_of(place_ref) == 0
    tails = jnp.concatenate(
        [jnp.where(straight, tail(groups[k]), tail(groups[k ^ 1])) for k in range(len(groups))], axis=0
    )
    counts, variance = tails[:, 0:1], tails[:, 1:2]
    mean = jnp.sum(left + right, axis=1, keepdims=True) * (1.0 / 256.0)
    left, right = left - mean, right - mean
    weights = 1.0 / variance
    weighted = weights * (counts - mean)
    mine = core_of(place_ref) == 0
    own = jnp.where(mine, left, right)
    half = jnp.where(mine, left[:, :64], left[:, 64:])
    out_ref[0:16] = dot3(halves(own), halves(own * weights), over_rows).reshape(16, 8, 128)
    out_ref[16:24] = dot3(halves(half), halves(right * weights), over_rows).reshape(8, 8, 128)
    forcing = [jnp.sum(part * weighted, axis=0, keepdims=True) for part in (left, right)]
    out_ref[24] = jnp.concatenate([*forcing, jnp.zeros((6, 128), F32)], axis=0)
    out_ref[25:] = jnp.zeros((out_ref.shape[0] - 25, 8, 128), F32)


def share_kernel(parts_ref, out_ref):
    total = jnp.sum(parts_ref[...], axis=0)
    out_ref[...] = jnp.broadcast_to(total[None], out_ref.shape)


def update_kernel(place_ref, live_hbm, pieces_ref, states_hbm, out_ref, states_ref, live_ref, sems):
    own_rows, members = states_ref.shape
    own = pl.ds(pl.multiple_of(link_of(place_ref) * own_rows, own_rows), own_rows)
    copies = (
        pltpu.make_async_copy(states_hbm.at[own], states_ref, sems.at[0]),
        pltpu.make_async_copy(live_hbm, live_ref, sems.at[1]),
    )
    for copy in copies:
        copy.start()
    by_core = pieces_ref[...].reshape(pieces_ref.shape[0] // 2, 2, 8, 128)
    first = by_core[0:16, 0].reshape(128, 128)
    last = by_core[0:16, 1].reshape(128, 128)
    across = jnp.concatenate([by_core[16:24, c].reshape(64, 128) for c in range(2)], axis=0)
    gram = jnp.concatenate(
        [jnp.concatenate([first, across], axis=1), jnp.concatenate([across.T, last], axis=1)], axis=0
    )
    forcing = jnp.concatenate([by_core[24, 0, 0:1], by_core[24, 0, 1:2]], axis=1)
    at = lambda dim: lax.broadcasted_iota(jnp.int32, (members, members), dim)
    diagonal = at(0) == at(1)
    identity = jnp.where(diagonal, 1.0, 0.0).astype(F32)
    forcing = jnp.sum(jnp.where(diagonal, forcing, 0.0), axis=1, keepdims=True)
    system = identity + gram * (1.0 / (members - 1.0))
    bound = jnp.max(jnp.sum(jnp.abs(system), axis=0, keepdims=True), axis=1, keepdims=True)
    root = system * (1.0 / bound)
    inverse = identity
    for sweep in range(NS_ITERS):
        if sweep == 0:
            middle = 1.5 * identity - 0.5 * root
            inverse = middle
        else:
            middle = 1.5 * identity - 0.5 * dot3(halves(inverse), halves(root))
        middle_halves = halves(middle)
        if sweep > 0:
            inverse = dot3(middle_halves, halves(inverse))
        if sweep < NS_ITERS - 1:
            root = dot3(halves(root), middle_halves)
    inner = jnp.sum(inverse * forcing, axis=0, keepdims=True)
    mean_weights = jnp.sum(inverse * inner, axis=1, keepdims=True) * (1.0 / (bound * (members - 1.0)))
    transform = inverse * lax.rsqrt(bound) + mean_weights
    transform += (1.0 - jnp.sum(transform, axis=0, keepdims=True)) * (1.0 / members)
    high, low = halves(transform)
    for copy in copies:
        copy.wait()
    own_blocks = own_rows // 128
    position = lax.broadcasted_iota(jnp.int32, (128, members), 0)
    for k in range(own_blocks):
        rows = slice(k * 128, k * 128 + 128)
        states = states_ref[rows, :]
        updated = dot(states, high) + dot(states, low)
        live = live_ref[link_of(place_ref) * own_blocks + k]
        out_ref[rows, :] = jnp.where(position < live, updated, states.astype(F32)).astype(BF16)


def all_to_all(x, axes):
    return lax.all_to_all(x, axes, split_axis=0, concat_axis=0, tiled=True)


def local(kernel, shape, operands, scalars=0):
    return pl.pallas_call(
        kernel,
        out_shape=jax.ShapeDtypeStruct(shape, F32),
        in_specs=[SMEM] * scalars + [VMEM] * operands,
        out_specs=VMEM,
        compiler_params=PARAMS,
        name=kernel.__name__,
    )


def per_device(background, live_counts, patterns, pattern_ids, link_targets, counts_obs, obs_var):
    states_dev, members = background.shape
    place = lax.axis_index(("zp", "zl", "c", "x")).astype(jnp.int32).reshape(1)
    ids, targets = (jnp.transpose(a, (2, 0, 1)) for a in (pattern_ids, link_targets))
    keep, send = term(place, ids, targets, live_counts, background, patterns[0])
    received = lax.ppermute(send, "c", [(0, 1), (1, 0)])
    of_chip = local(add_kernel, keep.shape, 2)(local(copy_kernel, keep.shape, 1)(keep), received)
    parts = all_to_all(of_chip, ("y", "zl"))
    own, other = pl.pallas_call(
        rows_kernel,
        out_shape=(jax.ShapeDtypeStruct((72, 128), F32),) * 2,
        in_specs=[SMEM, VMEM, VMEM, VMEM],
        out_specs=(VMEM, VMEM),
        compiler_params=PARAMS,
        name="rows",
    )(place, parts, counts_obs, obs_var)
    own += lax.ppermute(other, ("zq", "zp", "zl"), [(z, (z + (1 if z % 2 else -1)) % 16) for z in range(16)])
    column = lax.all_gather(own, ("zq", "zp", "c"))
    gram = local(gram_kernel, (32, 8, 128), 1, 1)(place, column)
    shared = local(share_kernel, (64, 8, 128), 1)(all_to_all(gram, ("x", "y", "zl")))
    pieces = all_to_all(shared, SLAB)
    own_rows = states_dev // lax.axis_size("x")
    return pl.pallas_call(
        update_kernel,
        out_shape=jax.ShapeDtypeStruct((own_rows, members), BF16),
        in_specs=[SMEM, HBM, VMEM, HBM],
        out_specs=VMEM,
        scratch_shapes=[
            pltpu.VMEM((own_rows, members), BF16),
            pltpu.SMEM(live_counts.shape, jnp.int32),
            pltpu.SemaphoreType.DMA((2,)),
        ],
        compiler_params=PARAMS,
        name="update",
    )(place, live_counts, pieces, background)


def solution(mesh):
    torus = Mesh(mesh.devices.reshape(4, 4, 2, 2, 2, 4), ("y", "zq", "zp", "zl", "c", "x"))
    return jax.shard_map(
        per_device,
        mesh=torus,
        in_specs=(
            P(ORIG, None),
            P(ORIG),
            P("x", ORIG, None, None),
            P("x", ORIG, None),
            P("x", ORIG, None),
            P("x", ORIG),
            P("x", ORIG),
        ),
        out_specs=P((*ORIG, "x"), None),
        check_vma=False,
    )
```

```python
import jax
import jax.numpy as jnp
from jax import lax
from jax.experimental import pallas as pl
from jax.experimental.pallas import tpu as pltpu
from jax.sharding import Mesh
from jax.sharding import PartitionSpec as P

NLB = 8
NS_ITERS = 4
F32 = jnp.float32
BF16 = jnp.bfloat16
ORIG = ("y", "zq", "zp", "zl", "c")
SLAB = ("x", "y", "zl", "c")
VMEM = pl.BlockSpec(memory_space=pltpu.VMEM)
SMEM = pl.BlockSpec(memory_space=pltpu.SMEM)
HBM = pl.BlockSpec(memory_space=pltpu.HBM)
DEPTH = 4
WHOLE = pltpu.CompilerParams(vmem_limit_bytes=58 * 2**20)
PARAMS = pltpu.CompilerParams(vmem_limit_bytes=40 * 2**20)


def halves(a):
    high = a.astype(BF16)
    return high, (a - high.astype(F32)).astype(BF16)


def dot(a, b):
    return jnp.dot(a, b, preferred_element_type=F32)


def dot3(a, b, dot=dot):
    (ah, al), (bh, bl) = a, b
    return dot(ah, bh) + (dot(ah, bl) + dot(al, bh))


def over_rows(a, b):
    return lax.dot_general(a, b, (((0,), (0,)), ((), ())), preferred_element_type=F32)


def link_of(place_ref):
    return place_ref[0] & 3


def core_of(place_ref):
    return jnp.right_shift(place_ref[0], 2) & 1


def side_of(place_ref):
    return jnp.right_shift(place_ref[0], 3) & 1


def pair_of(place_ref):
    return jnp.right_shift(place_ref[0], 4) & 1


def term_kernel(
    place_ref, ids_hbm, targets_hbm, live_hbm, states_hbm, tiles_hbm, keep_ref, send_ref,
    ids_ref, targets_ref, live_ref, states_ref, tiles_ref, order_ref, list_ref, sems,
):
    slots, _, blocks = ids_ref.shape
    stored, link_rows, block_rows = tiles_ref.shape
    states_dev, members = states_hbm.shape
    entries = slots * blocks
    steps = (entries + NLB * (DEPTH - 1)) // DEPTH
    empty = float(blocks * stored)
    copies = [
        pltpu.make_async_copy(there, here, sems.at[i])
        for i, (there, here) in enumerate(
            (
                (ids_hbm, ids_ref),
                (targets_hbm, targets_ref),
                (live_hbm, live_ref),
                (states_hbm, states_ref.at[pl.ds(0, states_dev)]),
                (tiles_hbm, tiles_ref),
            )
        )
    ]
    for copy in copies:
        copy.start()
    keep_ref[...] = jnp.zeros_like(keep_ref)
    send_ref[...] = jnp.zeros_like(send_ref)
    states_ref[states_dev:, :] = jnp.zeros((block_rows, members), BF16)
    iota = lambda shape, dim: lax.broadcasted_iota(jnp.int32, shape, dim)
    square = (entries, entries)
    diagonal = iota(square, 0) == iota(square, 1)
    before = jnp.where(iota(square, 0) < iota(square, 1), 1.0, 0.0).astype(BF16)
    column = lambda row: jnp.sum(jnp.where(diagonal, row, 0.0), axis=1, keepdims=True)
    row = lambda a: jnp.concatenate([a[t] for t in range(slots)], axis=1).astype(F32)
    copies[0].wait()
    copies[1].wait()
    target = row(targets_ref[...])
    code = target * 1024.0 + row(iota(ids_ref.shape, 2) * stored + ids_ref[...])
    hits = jnp.where(iota((NLB, entries), 0).astype(F32) == target, 1.0, 0.0)
    rank = dot(hits.astype(BF16), before)
    needed = jnp.floor((jnp.sum(hits, axis=1, keepdims=True) + (DEPTH - 1)) * (1.0 / DEPTH)) * DEPTH
    starts = [jnp.zeros((1, 1), F32)]
    for j in range(NLB - 1):
        starts.append(starts[j] + needed[j : j + 1])
    places = jnp.sum(hits * (rank + jnp.concatenate(starts, axis=0)), axis=0, keepdims=True)
    put = column(places) == iota((entries, order_ref.shape[1]), 1).astype(F32)
    order = empty + jnp.sum(jnp.where(put, column(code) - empty, 0.0), axis=0, keepdims=True)
    order_ref[...] = order.astype(jnp.int32)
    ordered = pltpu.make_async_copy(order_ref, list_ref, sems.at[5])
    ordered.start()

    copies[2].wait()
    copies[3].wait()
    position = lax.broadcasted_iota(jnp.int32, (block_rows, members), 0)
    for b in range(blocks):
        rows = slice(b * block_rows, (b + 1) * block_rows)
        living = (position < live_ref[b]).astype(F32).astype(BF16)
        states_ref[rows, :] = states_ref[rows, :] * living
    copies[4].wait()
    ordered.wait()

    pair = pair_of(place_ref)

    def run(by_core):
        def step(i, carry):
            codes = [list_ref[0, i * DEPTH + k] for k in range(DEPTH)]
            tiles, states = [], []
            for code in codes:
                first = pl.multiple_of((jnp.right_shift(code, 5) & 31) * block_rows, block_rows)
                tiles.append(tiles_ref[code & 31])
                states.append(states_ref[pl.ds(first, block_rows), :])
            product = dot(jnp.concatenate(tiles, axis=1), jnp.concatenate(states, axis=0))
            target = jnp.right_shift(codes[0], 10)
            chunk = jnp.right_shift(target, 1) * 2
            for g in range(16):
                h, p, l, c = g // 8, (g // 4) % 2, (g // 2) % 2, g % 2
                at = pl.ds(pl.multiple_of((target & 1) * 32 + h * 16 + l * 8, 8), 8)
                by_core[c][chunk + (p ^ pair), at, :] += product[g * 8 : g * 8 + 8]
            return carry

        lax.fori_loop(0, steps, step, 0, unroll=steps)

    @pl.when(core_of(place_ref) == 0)
    def _():
        run((keep_ref, send_ref))

    @pl.when(core_of(place_ref) == 1)
    def _():
        run((send_ref, keep_ref))


def term(place, ids, targets, live, states, tiles):
    slots, _, blocks = ids.shape
    states_dev, members = states.shape
    places = -(-(slots * blocks + NLB * (DEPTH - 1)) // 128) * 128
    half = jax.ShapeDtypeStruct((8, 64, members), F32)
    return pl.pallas_call(
        term_kernel,
        out_shape=(half, half),
        in_specs=[SMEM] + [HBM] * 5,
        out_specs=(VMEM, VMEM),
        scratch_shapes=[
            pltpu.VMEM(ids.shape, jnp.int32),
            pltpu.VMEM(ids.shape, jnp.int32),
            pltpu.SMEM(live.shape, jnp.int32),
            pltpu.VMEM((states_dev + tiles.shape[2], members), BF16),
            pltpu.VMEM(tiles.shape, BF16),
            pltpu.VMEM((1, places), jnp.int32),
            pltpu.SMEM((1, places), jnp.int32),
            pltpu.SemaphoreType.DMA((6,)),
        ],
        compiler_params=WHOLE,
        name="term",
    )(place, ids, targets, live, states, tiles)


def as_column(ref):
    count = ref.shape[1]
    at = lambda dim: lax.broadcasted_iota(jnp.int32, (count, count), dim)
    return jnp.sum(jnp.where(at(0) == at(1), ref[...], 0.0), axis=1, keepdims=True)


def copy_kernel(a_ref, out_ref):
    out_ref[...] = a_ref[...]


def add_kernel(a_ref, b_ref, out_ref):
    out_ref[...] = a_ref[...] + b_ref[...]


def rows_kernel(place_ref, parts_ref, counts_ref, var_ref, keep_ref, send_ref):
    total = jnp.sum(parts_ref[...], axis=0)
    rows, members = total.shape
    by_pair = total.reshape(rows // 16, 2, 8, members)
    first, second = (by_pair[:, p].reshape(rows // 2, members) for p in range(2))
    mine = side_of(place_ref) == 0
    lane = lax.broadcasted_iota(jnp.int32, (8, 128), 1)
    counts, variance = as_column(counts_ref), as_column(var_ref)
    tail = jnp.where(lane == 0, counts, jnp.where(lane == 1, variance, 0.0))
    for ref, at, below in ((keep_ref, mine, tail), (send_ref, jnp.logical_not(mine), jnp.zeros_like(tail))):
        chosen = jnp.where(at, first, second)
        ref[0 : rows // 2, :] = chosen[:, :128]
        ref[rows // 2 : rows, :] = chosen[:, 128:]
        ref[rows:, :] = below


def gram_kernel(place_ref, parts_ref, out_ref):
    rows = (parts_ref.shape[1] - 8) // 2
    quads = parts_ref.shape[0] // 4
    groups = [[(2 * k + p) * 2 + c for k in range(quads)] for c in range(2) for p in range(2)]

    def whole(first):
        return jnp.concatenate([sum(parts_ref[m, first : first + rows, :] for m in g) for g in groups], axis=0)

    left, right = whole(0), whole(rows)
    tail = lambda g: jnp.concatenate([parts_ref[m, 2 * rows :, :] for m in g], axis=0)
    straight = side_of(place_ref) == 0
    tails = jnp.concatenate(
        [jnp.where(straight, tail(groups[k]), tail(groups[k ^ 1])) for k in range(len(groups))], axis=0
    )
    counts, variance = tails[:, 0:1], tails[:, 1:2]
    mean = jnp.sum(left + right, axis=1, keepdims=True) * (1.0 / 256.0)
    left, right = left - mean, right - mean
    weights = 1.0 / variance
    weighted = weights * (counts - mean)
    mine = core_of(place_ref) == 0
    own = jnp.where(mine, left, right)
    half = jnp.where(mine, left[:, :64], left[:, 64:])
    out_ref[0:16] = dot3(halves(own), halves(own * weights), over_rows).reshape(16, 8, 128)
    out_ref[16:24] = dot3(halves(half), halves(right * weights), over_rows).reshape(8, 8, 128)
    forcing = [jnp.sum(part * weighted, axis=0, keepdims=True) for part in (left, right)]
    out_ref[24] = jnp.concatenate([*forcing, jnp.zeros((6, 128), F32)], axis=0)
    out_ref[25:] = jnp.zeros((out_ref.shape[0] - 25, 8, 128), F32)


def share_kernel(parts_ref, out_ref):
    total = jnp.sum(parts_ref[...], axis=0)
    out_ref[...] = jnp.broadcast_to(total[None], out_ref.shape)


def update_kernel(place_ref, live_hbm, pieces_ref, states_hbm, out_ref, states_ref, live_ref, sems):
    own_rows, members = states_ref.shape
    own = pl.ds(pl.multiple_of(link_of(place_ref) * own_rows, own_rows), own_rows)
    copies = (
        pltpu.make_async_copy(states_hbm.at[own], states_ref, sems.at[0]),
        pltpu.make_async_copy(live_hbm, live_ref, sems.at[1]),
    )
    for copy in copies:
        copy.start()
    by_core = pieces_ref[...].reshape(pieces_ref.shape[0] // 2, 2, 8, 128)
    first = by_core[0:16, 0].reshape(128, 128)
    last = by_core[0:16, 1].reshape(128, 128)
    across = jnp.concatenate([by_core[16:24, c].reshape(64, 128) for c in range(2)], axis=0)
    gram = jnp.concatenate(
        [jnp.concatenate([first, across], axis=1), jnp.concatenate([across.T, last], axis=1)], axis=0
    )
    forcing = jnp.concatenate([by_core[24, 0, 0:1], by_core[24, 0, 1:2]], axis=1)
    at = lambda dim: lax.broadcasted_iota(jnp.int32, (members, members), dim)
    diagonal = at(0) == at(1)
    identity = jnp.where(diagonal, 1.0, 0.0).astype(F32)
    forcing = jnp.sum(jnp.where(diagonal, forcing, 0.0), axis=1, keepdims=True)
    system = identity + gram * (1.0 / (members - 1.0))
    bound = jnp.max(jnp.sum(jnp.abs(system), axis=0, keepdims=True), axis=1, keepdims=True)
    root = system * (1.0 / bound)
    inverse = identity
    for sweep in range(NS_ITERS):
        if sweep == 0:
            middle = 1.5 * identity - 0.5 * root
            inverse = middle
        else:
            middle = 1.5 * identity - 0.5 * dot3(halves(inverse), halves(root))
        middle_halves = halves(middle)
        if sweep > 0:
            inverse = dot3(middle_halves, halves(inverse))
        if sweep < NS_ITERS - 1:
            root = dot3(halves(root), middle_halves)
    inner = jnp.sum(inverse * forcing, axis=0, keepdims=True)
    mean_weights = jnp.sum(inverse * inner, axis=1, keepdims=True) * (1.0 / (bound * (members - 1.0)))
    transform = inverse * lax.rsqrt(bound) + mean_weights
    transform += (1.0 - jnp.sum(transform, axis=0, keepdims=True)) * (1.0 / members)
    high, low = halves(transform)
    for copy in copies:
        copy.wait()
    own_blocks = own_rows // 128
    position = lax.broadcasted_iota(jnp.int32, (128, members), 0)
    for k in range(own_blocks):
        rows = slice(k * 128, k * 128 + 128)
        states = states_ref[rows, :]
        updated = dot(states, high) + dot(states, low)
        live = live_ref[link_of(place_ref) * own_blocks + k]
        out_ref[rows, :] = jnp.where(position < live, updated, states.astype(F32)).astype(BF16)


def all_to_all(x, axes):
    return lax.all_to_all(x, axes, split_axis=0, concat_axis=0, tiled=True)


def local(kernel, shape, operands, scalars=0):
    return pl.pallas_call(
        kernel,
        out_shape=jax.ShapeDtypeStruct(shape, F32),
        in_specs=[SMEM] * scalars + [VMEM] * operands,
        out_specs=VMEM,
        compiler_params=PARAMS,
        name=kernel.__name__,
    )


def per_device(background, live_counts, patterns, pattern_ids, link_targets, counts_obs, obs_var):
    states_dev, members = background.shape
    place = lax.axis_index(("zp", "zl", "c", "x")).astype(jnp.int32).reshape(1)
    ids, targets = (jnp.transpose(a, (2, 0, 1)) for a in (pattern_ids, link_targets))
    keep, send = term(place, ids, targets, live_counts, background, patterns[0])
    received = lax.ppermute(send, "c", [(0, 1), (1, 0)])
    of_chip = local(add_kernel, keep.shape, 2)(local(copy_kernel, keep.shape, 1)(keep), received)
    parts = all_to_all(of_chip, ("y", "zl"))
    own, other = pl.pallas_call(
        rows_kernel,
        out_shape=(jax.ShapeDtypeStruct((72, 128), F32),) * 2,
        in_specs=[SMEM, VMEM, VMEM, VMEM],
        out_specs=(VMEM, VMEM),
        compiler_params=PARAMS,
        name="rows",
    )(place, parts, counts_obs, obs_var)
    own += lax.ppermute(other, ("zq", "zp", "zl"), [(z, (z + (1 if z % 2 else -1)) % 16) for z in range(16)])
    column = lax.all_gather(own, ("zq", "zp", "c"))
    gram = local(gram_kernel, (32, 8, 128), 1, 1)(place, column)
    shared = local(share_kernel, (64, 8, 128), 1)(all_to_all(gram, ("x", "y", "zl")))
    pieces = all_to_all(shared, SLAB)
    own_rows = states_dev // lax.axis_size("x")
    return pl.pallas_call(
        update_kernel,
        out_shape=jax.ShapeDtypeStruct((own_rows, members), BF16),
        in_specs=[SMEM, HBM, VMEM, HBM],
        out_specs=VMEM,
        scratch_shapes=[
            pltpu.VMEM((own_rows, members), BF16),
            pltpu.SMEM(live_counts.shape, jnp.int32),
            pltpu.SemaphoreType.DMA((2,)),
        ],
        compiler_params=PARAMS,
        name="update",
    )(place, live_counts, pieces, background)


def solution(mesh):
    torus = Mesh(mesh.devices.reshape(4, 4, 2, 2, 2, 4), ("y", "zq", "zp", "zl", "c", "x"))
    return jax.shard_map(
        per_device,
        mesh=torus,
        in_specs=(
            P(ORIG, None),
            P(ORIG),
            P("x", ORIG, None, None),
            P("x", ORIG, None),
            P("x", ORIG, None),
            P("x", ORIG),
            P("x", ORIG),
        ),
        out_specs=P((*ORIG, "x"), None),
        check_vma=False,
    )
```
